32 devices in a mesh: seq: 8 (over z, x), head: 4 (over y, core).
Axes of the slice: x: 2, y: 2, z: 4, core: 2. Of those that a mesh axis runs over, the one named last changes fastest.
Arguments:
- queries: bfloat16 [2048, 24, 128], P('seq', 'head'), may hold values from -6 to 6
- key_vectors: bfloat16 [2048, 24, 128], P('seq', 'head'), may hold values from -6 to 6
- values: bfloat16 [2048, 24, 128], P('seq', 'head'), may hold values from -6 to 6
- out_grad: bfloat16 [2048, 24, 128], P('seq', 'head'), may hold values from -6 to 6
- ssm_input: bfloat16 [2048, 48, 128], P('seq', 'head'), may hold values from -6 to 6
- ssm_out_grad: bfloat16 [2048, 48, 128], P('seq', 'head'), may hold values from -1.5 to 1.5
- step_sizes: float32 [2048, 48], P('seq', 'head'), may hold values from 0 to 2, as said below
- decay_rates: float32 [48], P('head'), may hold values from -1 to 0, as said below
- skip_gains: float32 [48], P('head'), may hold values from 0.5 to 1.5
- bc_rows: bfloat16 [2048, 128], P('seq'), may hold values from -0.75 to 0.75
- saved_states: float32 [8, 48, 64, 128], P('seq', 'head'), may hold values from -6 to 6
Outputs:
- query_grad: bfloat16 [2048, 24, 128], P('seq', 'head')
- key_grad: bfloat16 [2048, 24, 128], P('seq', 'head')
- value_grad: bfloat16 [2048, 24, 128], P('seq', 'head')
- grad_inputs: bfloat16 [2048, 48, 128], P('seq', 'head')
- grad_steps: float32 [2048, 48], P('seq', 'head')
- grad_bc: float32 [2048, 128], P(('seq', 'head'))
- grad_decay: float32 [48], P('head')
- grad_skip: float32 [48], P('head')
The draws below stay inside these ranges and needn't reach their ends.
Inputs may be any that keep to these rules, and one draw needn't show every extreme that they name: `step_sizes`: positive. `decay_rates`: negative.
All inputs are finite; a program needn't handle non-finite values.
Results may differ from the reference program's by a relative error of at most 0.0095.
Values may be sent and summed in bfloat16 or wider, within the bound.
No kernel may reach another device: no remote copies, remote signals or barrier semaphores. Data moves between devices by JAX's collectives and lax.ppermute only.
A program may use at most 192 MiB of HBM per device.

```python
import jax
import jax.numpy as jnp
from jax import lax

AHEADS = 24
HD = 128
STATE_SPACE_SETS = 48
MP = 128
NSTATE = 64
WINDOW = 1024
GROUP = 256
TOK_DEV = 256
SEQUENCE_LENGTH = 2048
SAVES = 8


def attention_pair(key):
    base_key = jax.random.fold_in(key, 11)
    key_q, key_k = jax.random.split(base_key, 2)
    shape_all = (SEQUENCE_LENGTH, AHEADS, HD)
    query_draw = jax.random.normal(key_q, shape_all, jnp.float32)
    key_draw = jax.random.normal(key_k, shape_all, jnp.float32)
    return (jnp.clip(query_draw, -6.0, 6.0), jnp.clip(key_draw, -6.0, 6.0))


def draw_queries(key, part):
    return attention_pair(key)[0].astype(jnp.bfloat16)


def draw_key_vectors(key, part):
    return attention_pair(key)[1].astype(jnp.bfloat16)


def draw_decay_rates(key, part):
    key_slow, key_fast, key_span = jax.random.split(jax.random.fold_in(key, 23), 3)
    slow_heads = jax.random.bernoulli(key_slow, 0.5, (STATE_SPACE_SETS,))
    fast_rate = -jax.random.uniform(key_fast, (STATE_SPACE_SETS,), jnp.float32, 0.4, 0.8)
    slow_rate = -jax.random.uniform(key_span, (STATE_SPACE_SETS,), jnp.float32, 0.5, 1.0) * (20.0 / SEQUENCE_LENGTH)
    return jnp.where(slow_heads, slow_rate, fast_rate)


def draw_step_sizes(key, part):
    key_rough, key_block, key_place, key_amount = jax.random.split(jax.random.fold_in(key, 31), 4)
    approximate_guess = jax.random.uniform(key_rough, (SEQUENCE_LENGTH, STATE_SPACE_SETS), jnp.float32, 0.5, 1.5)
    segmented_lines = jnp.exp(jax.random.uniform(key_block, (SEQUENCE_LENGTH // TOK_DEV, 1, STATE_SPACE_SETS), jnp.float32, -0.4, 0.4))
    segmented_lines = jnp.broadcast_to(segmented_lines, (SEQUENCE_LENGTH // TOK_DEV, TOK_DEV, STATE_SPACE_SETS)).reshape(SEQUENCE_LENGTH, STATE_SPACE_SETS)
    location_series = jax.random.randint(key_place, (3, STATE_SPACE_SETS), 0, SEQUENCE_LENGTH)
    quantity_series = jax.random.uniform(key_amount, (3, STATE_SPACE_SETS), jnp.float32, 2.0, 6.0)
    vertical_position = jnp.arange(SEQUENCE_LENGTH)[:, None]
    packet_clusters = jnp.zeros((SEQUENCE_LENGTH, STATE_SPACE_SETS), jnp.float32)
    for numeric_quantity in range(3):
        packet_clusters = packet_clusters + jnp.where(vertical_position == location_series[numeric_quantity][None, :], quantity_series[numeric_quantity][None, :], 0.0)
    return 0.05 * approximate_guess * segmented_lines + 0.05 * packet_clusters


def block_scale(key, shape, cuts, least, high):
    def one(axis_at, parts):
        draws = jax.random.uniform(jax.random.fold_in(jax.random.fold_in(key, 6), axis_at), (parts,), jnp.float32, least / len(cuts), high / len(cuts))
        return jnp.repeat(jnp.exp(draws), shape[axis_at] // parts).reshape((-1,) + (1,) * (len(shape) - axis_at - 1))

    factor_of = one(*cuts[0])
    for cut in cuts[1:]:
        factor_of = factor_of * one(*cut)
    return factor_of


def bell_draw(own_key, shape, width, limit, cuts=(), kind=jnp.bfloat16):
    drawn = width * jax.random.normal(own_key, shape, jnp.float32)
    if cuts:
        drawn = drawn * block_scale(own_key, shape, cuts, -0.22, 0.18)
    return jnp.clip(drawn, -limit, limit).astype(kind)


def setup_inputs(seed: int = 0) -> dict:
    streams_of = jax.random.split(jax.random.key(seed), 12)
    queries = draw_queries(jax.random.fold_in(streams_of[11], 71), 0)
    key_vectors = draw_key_vectors(jax.random.fold_in(streams_of[11], 71), 0)
    values = bell_draw(streams_of[2], (SEQUENCE_LENGTH, AHEADS, HD), 1.0, 6.0, ((0, 8), (1, 4)))
    out_grad = bell_draw(streams_of[3], (SEQUENCE_LENGTH, AHEADS, HD), 1.0, 6.0, ((0, 8), (1, 4)))
    ssm_input = bell_draw(streams_of[4], (SEQUENCE_LENGTH, STATE_SPACE_SETS, MP), 1.0, 6.0, ((0, 8), (1, 4)))
    ssm_out_grad = bell_draw(streams_of[5], (SEQUENCE_LENGTH, STATE_SPACE_SETS, MP), 0.25, 1.5, ((0, 8), (1, 4)))
    step_sizes = draw_step_sizes(jax.random.fold_in(streams_of[11], 71), 0)
    decay_rates = draw_decay_rates(jax.random.fold_in(streams_of[11], 71), 0)
    skip_gains = jnp.clip(0.5 + 1.0 * jax.random.uniform(streams_of[8], (STATE_SPACE_SETS,), jnp.float32) ** block_scale(streams_of[8], (STATE_SPACE_SETS,), ((0, 4),), -0.2, 0.2), 0.5, 1.5)
    bc_rows = bell_draw(streams_of[9], (SEQUENCE_LENGTH, 2 * NSTATE), 0.125, 0.75, ((0, 8),))
    saved_states = bell_draw(streams_of[10], (SAVES, STATE_SPACE_SETS, NSTATE, MP), 1.0, 6.0, ((0, 8), (1, 4)), jnp.float32)
    return {"queries": queries, "key_vectors": key_vectors, "values": values, "out_grad": out_grad, "ssm_input": ssm_input, "ssm_out_grad": ssm_out_grad, "step_sizes": step_sizes, "decay_rates": decay_rates, "skip_gains": skip_gains, "bc_rows": bc_rows, "saved_states": saved_states}


TOP_PRECISION = lax.Precision.HIGHEST

def attention_grads(queries, key_vectors, values, out_grad):
    count = TOK_DEV
    extent = WINDOW + TOK_DEV
    blocks_total = SEQUENCE_LENGTH // TOK_DEV
    scaling_factor = HD ** (-0.5)
    padding = jnp.zeros((WINDOW, AHEADS, HD), queries.dtype)
    keys_pad = jnp.concatenate([padding, key_vectors], axis=0)
    values_pad = jnp.concatenate([padding, values], axis=0)
    row_ids = lax.broadcasted_iota(jnp.int32, (count, extent), 0)
    col_ids = lax.broadcasted_iota(jnp.int32, (count, extent), 1)

    def block_step(carry, block_id):
        key_acc, value_acc = carry
        begin = (block_id * count).astype(jnp.int32)
        query_tile = lax.dynamic_slice_in_dim(queries, begin, count, 0).astype(jnp.float32)
        gradient_block = lax.dynamic_slice_in_dim(out_grad, begin, count, 0).astype(jnp.float32)
        key_tile = lax.dynamic_slice_in_dim(keys_pad, begin, extent, 0).astype(jnp.float32)
        value_tile = lax.dynamic_slice_in_dim(values_pad, begin, extent, 0).astype(jnp.float32)
        usable = (col_ids > row_ids) & (col_ids <= WINDOW + row_ids) & (col_ids + begin >= WINDOW)
        score_matrix = jnp.einsum('uoh,soh->ous', query_tile, key_tile, precision=TOP_PRECISION) * scaling_factor
        score_matrix = jnp.where(usable[None], score_matrix, -jnp.inf)
        row_max = lax.optimization_barrier(jnp.max(score_matrix, axis=2, keepdims=True))
        log_total = row_max + jnp.log(lax.optimization_barrier(jnp.sum(jnp.exp(score_matrix - row_max), axis=2, keepdims=True)))
        probs = jnp.exp(score_matrix - log_total)
        probs_reduced = probs.astype(jnp.bfloat16).astype(jnp.float32)
        probs_gradient = jnp.einsum('uoh,soh->ous', gradient_block, value_tile, precision=TOP_PRECISION)
        delta_row = lax.optimization_barrier(jnp.sum(probs * probs_gradient, axis=2, keepdims=True))
        scores_gradient = (probs * (probs_gradient - delta_row) * scaling_factor).astype(jnp.bfloat16).astype(jnp.float32)
        query_gradient = jnp.einsum('uzs,suy->zuy', scores_gradient, key_tile, precision=TOP_PRECISION)
        key_gradient = jnp.einsum('wut,uwc->twc', scores_gradient, query_tile, precision=TOP_PRECISION)
        value_gradient = jnp.einsum('wut,uwc->twc', probs_reduced, gradient_block, precision=TOP_PRECISION)
        key_acc = lax.dynamic_update_slice_in_dim(key_acc, lax.dynamic_slice_in_dim(key_acc, begin, extent, 0) + key_gradient, begin, 0)
        value_acc = lax.dynamic_update_slice_in_dim(value_acc, lax.dynamic_slice_in_dim(value_acc, begin, extent, 0) + value_gradient, begin, 0)
        return ((key_acc, value_acc), query_gradient.astype(jnp.bfloat16))
    zero_acc = jnp.zeros((WINDOW + SEQUENCE_LENGTH, AHEADS, HD), jnp.float32)
    (key_acc, value_acc), q_grads = lax.scan(block_step, (zero_acc, zero_acc), jnp.arange(blocks_total, dtype=jnp.int32))
    query_grad = q_grads.reshape(SEQUENCE_LENGTH, AHEADS, HD)
    return (query_grad, key_acc[WINDOW:].astype(jnp.bfloat16), value_acc[WINDOW:].astype(jnp.bfloat16))

def group_loss(inputs_part, steps_part, bc_part, decay_rates, skip_gains, start_state, incoming, out_part):
    log_decay = steps_part * decay_rates[None, :]
    cumulative = jnp.cumsum(log_decay, axis=0)
    last_sum = cumulative[-1]
    b_rows = bc_part[:, :NSTATE]
    c_rows = bc_part[:, NSTATE:]
    row_ids = lax.broadcasted_iota(jnp.int32, (GROUP, GROUP), 0)
    col_ids = lax.broadcasted_iota(jnp.int32, (GROUP, GROUP), 1)
    in_lower = (col_ids <= row_ids)[None]
    spread = cumulative.T[:, :, None] - cumulative.T[:, None, :]
    lower_decay = jnp.where(in_lower, jnp.exp(jnp.where(in_lower, spread, 0.0)), 0.0)
    inner_cb = jnp.dot(c_rows, b_rows.T, precision=TOP_PRECISION)
    driven = steps_part[:, :, None] * inputs_part
    outputs = jnp.exp(cumulative)[:, :, None] * jnp.einsum('tn,hnp->thp', c_rows, start_state, precision=TOP_PRECISION)
    outputs = outputs + jnp.einsum('hts,shp->thp', lower_decay * inner_cb[None], driven, precision=TOP_PRECISION)
    outputs = outputs + skip_gains[None, :, None] * inputs_part
    tail_decay = jnp.exp(last_sum[None, :] - cumulative)
    final_state = jnp.exp(last_sum)[:, None, None] * start_state
    final_state = final_state + jnp.einsum('shp,sn->hnp', driven * tail_decay[:, :, None], b_rows, precision=TOP_PRECISION)
    return jnp.sum(outputs * out_part) + jnp.sum(incoming * final_state)

def ssm_grads(ssm_input, ssm_out_grad, step_sizes, decay_rates, skip_gains, bc_rows, saved_states):
    pieces = SEQUENCE_LENGTH // GROUP
    inputs_f = ssm_input.astype(jnp.float32).reshape(pieces, GROUP, STATE_SPACE_SETS, MP)
    grads_f = ssm_out_grad.astype(jnp.float32).reshape(pieces, GROUP, STATE_SPACE_SETS, MP)
    steps_f = step_sizes.reshape(pieces, GROUP, STATE_SPACE_SETS)
    bc_f = bc_rows.astype(jnp.float32).reshape(pieces, GROUP, 2 * NSTATE)
    gradient = jax.grad(group_loss, argnums=(0, 1, 2, 3, 4, 5))

    def backward_step(carry, item):
        incoming, decay_sum, skip_sum = carry
        inputs_part, out_part, steps_part, bc_part, start_state = item
        g_inputs, g_steps, g_bc, g_decay, g_skip, g_start = gradient(inputs_part, steps_part, bc_part, decay_rates, skip_gains, start_state, incoming, out_part)
        return ((g_start, decay_sum + g_decay, skip_sum + g_skip), (g_inputs, g_steps, g_bc))
    initial = (jnp.zeros((STATE_SPACE_SETS, NSTATE, MP), jnp.float32), jnp.zeros((STATE_SPACE_SETS,), jnp.float32), jnp.zeros((STATE_SPACE_SETS,), jnp.float32))
    (unused, decay_sum, skip_sum), (g_inputs, g_steps, g_bc) = lax.scan(backward_step, initial, (inputs_f, grads_f, steps_f, bc_f, saved_states), reverse=True)
    grad_inputs = g_inputs.reshape(SEQUENCE_LENGTH, STATE_SPACE_SETS, MP).astype(jnp.bfloat16)
    grad_steps = g_steps.reshape(SEQUENCE_LENGTH, STATE_SPACE_SETS)
    grad_bc = g_bc.reshape(SEQUENCE_LENGTH, 2 * NSTATE)
    return (grad_inputs, grad_steps, grad_bc, decay_sum, skip_sum)

def reference(queries, key_vectors, values, out_grad, ssm_input, ssm_out_grad, step_sizes, decay_rates, skip_gains, bc_rows, saved_states):
    query_grad, key_grad, value_grad = attention_grads(queries, key_vectors, values, out_grad)
    grad_inputs, grad_steps, grad_bc, grad_decay, grad_skip = ssm_grads(ssm_input, ssm_out_grad, step_sizes, decay_rates, skip_gains, bc_rows, saved_states)
    return (query_grad, key_grad, value_grad, grad_inputs, grad_steps, grad_bc, grad_decay, grad_skip)
```

```python
import functools
import math

import jax
import jax.numpy as jnp
from jax import lax
from jax.experimental import pallas as pl
from jax.experimental.pallas import tpu as pltpu
from jax.sharding import PartitionSpec as P

NSTATE = 64
WINDOW = 1024
LOG2E = math.log2(math.e)
NEVER = -1e30
EXACT = lax.Precision.HIGHEST
F32 = jnp.float32
BF16 = jnp.bfloat16
VMEM_BYTES = 48 * 1024 * 1024


def dot(left, right, contract, precision=None):
    return lax.dot_general(
        left, right, (contract, ((), ())), precision=precision, preferred_element_type=F32
    )


NT = ((1,), (1,))
NN = ((1,), (0,))
TN = ((0,), (0,))


def moved(value, steps):
    count = lax.axis_size("seq")
    pairs = [(at, at + steps) for at in range(count) if 0 <= at + steps < count]
    return lax.ppermute(value, "seq", pairs)


def swapped(value):
    count = lax.axis_size("seq")
    return lax.ppermute(value, "seq", [(at, at ^ 1) for at in range(count)])


def vmem(count):
    return [pl.BlockSpec(memory_space=pltpu.VMEM)] * count


def call(body, outs, ins, flops, scratch=(), smem=0, name=None):
    whole = sum(math.prod(v.shape) * v.dtype.itemsize for v in (*ins, *outs))
    specs = [pl.BlockSpec(memory_space=pltpu.SMEM)] * smem + vmem(len(ins) - smem)
    return pl.pallas_call(
        body,
        out_shape=outs,
        in_specs=specs,
        out_specs=vmem(len(outs)),
        scratch_shapes=list(scratch),
        compiler_params=pltpu.CompilerParams(vmem_limit_bytes=VMEM_BYTES),
        cost_estimate=pl.CostEstimate(flops=flops, bytes_accessed=whole, transcendentals=0),
        name=name,
    )(*ins)


def shape(dims, dtype):
    return jax.ShapeDtypeStruct(dims, dtype)


def block_mask(distance, reach, tokens):
    keys = lax.broadcasted_iota(jnp.int32, (tokens, tokens), 0)
    rows = lax.broadcasted_iota(jnp.int32, (tokens, tokens), 1)
    if distance == 0:
        return keys <= rows
    if distance == reach:
        return keys > rows
    return None


def scores(key_block, query_block, mask, factor, bias=None):
    value = dot(key_block, query_block, NT) * factor
    if bias is not None:
        value = value + bias
    if mask is not None:
        value = jnp.where(mask, value, NEVER)
    return value


def place_pairs(place, mine, theirs, target, first):
    for step in range(len(mine)):
        target[first + 2 * step + place] = mine[step][...]
        target[first + 2 * step + 1 - place] = theirs[step][...]


def stats_body(reach, *refs):
    where_ref = refs[0]
    hops = reach // 2
    keys = refs[1 : 1 + 2 * (hops + 1)]
    qg_mine, qg_theirs, stats_ref, kv, qg = refs[1 + 2 * (hops + 1) :]
    place, pair = where_ref[0], where_ref[1]
    place_pairs(place, keys[0::2], keys[1::2], kv, 0)
    place_pairs(place, [qg_mine], [qg_theirs], qg, 0)
    heads, tokens, width = kv.shape[2:]
    factor = width ** (-0.5) * LOG2E
    masks = {0: block_mask(0, reach, tokens), reach: block_mask(reach, reach, tokens)}
    biases = [jnp.where(pair >= hops - hop, 0.0, NEVER) for hop in range(hops)] + [None]
    for head in range(heads):
        for a in range(2):
            q, g = qg[a, 0, head], qg[a, 1, head]
            top = total = delta = None
            for j in range(a + reach, a - 1, -1):
                s = scores(kv[j, 0, head], q, masks.get(a + reach - j), factor, biases[j // 2])
                dp = dot(kv[j, 1, head], g, NT)
                best = jnp.max(s, axis=0, keepdims=True)
                if top is not None:
                    best = jnp.maximum(top, best)
                p = jnp.exp2(s - best)
                own_total = jnp.sum(p, axis=0, keepdims=True)
                own_delta = jnp.sum(p * dp, axis=0, keepdims=True)
                if top is None:
                    total, delta = own_total, own_delta
                else:
                    fade = jnp.exp2(top - best)
                    total, delta = total * fade + own_total, delta * fade + own_delta
                top = best
            at = 2 * head + a
            stats_ref[0, at : at + 1, :] = top + jnp.log2(total)
            stats_ref[1, at : at + 1, :] = delta / total


def score_grads(key_block, value_block, q, g, lse, delta, mask, factor, scale, bias=None):
    p = jnp.exp2(scores(key_block, q, mask, factor, bias) - lse)
    dp = dot(value_block, g, NT)
    return p, (p * (dp - delta) * scale).astype(BF16)


def query_body(reach, *refs):
    where_ref = refs[0]
    hops = reach // 2
    keys = refs[1 : 1 + 2 * (hops + 1)]
    qg_mine, qg_theirs, stats_ref, dq_mine, dq_theirs, part, kv, qg, dq = refs[1 + 2 * (hops + 1) :]
    place, pair = where_ref[0], where_ref[1]
    place_pairs(place, keys[0::2], keys[1::2], kv, 0)
    place_pairs(place, [qg_mine], [qg_theirs], qg, 0)
    heads, tokens, width = kv.shape[2:]
    scale = width ** (-0.5)
    factor = scale * LOG2E
    masks = {0: block_mask(0, reach, tokens), reach: block_mask(reach, reach, tokens)}
    biases = [jnp.where(pair >= hops - hop, 0.0, NEVER) for hop in range(hops)] + [None]
    for head in range(heads):
        for a in range(2):
            q, g = qg[a, 0, head], qg[a, 1, head]
            at = 2 * head + a
            lse, delta = stats_ref[0, at : at + 1, :], stats_ref[1, at : at + 1, :]
            grad = None
            for j in range(a, a + reach + 1):
                key_block = kv[j, 0, head]
                p, ds = score_grads(
                    key_block, kv[j, 1, head], q, g, lse, delta,
                    masks.get(a + reach - j), factor, scale, biases[j // 2],
                )
                term = dot(ds, key_block, TN)
                grad = term if grad is None else grad + term
                own = j - reach
                if own >= 0:
                    dk, dv = dot(ds, q, NN), dot(p.astype(BF16), g, NN)
                    if a == own:
                        part[own, 0, head], part[own, 1, head] = dk, dv
                    if a > own:
                        part[own, 0, head] += dk
                        part[own, 1, head] += dv
            dq[a, head] = grad.astype(BF16)
    dq_mine[...] = dq[place]
    dq_theirs[...] = dq[1 - place]


def later_body(reach, *refs):
    where_ref = refs[0]
    hops = reach // 2
    own_mine, own_theirs = refs[1:3]
    rows = refs[3 : 3 + 2 * hops]
    stats = refs[3 + 2 * hops : 3 + 3 * hops]
    part, mine, theirs, kv, qg, out = refs[3 + 3 * hops :]
    place = where_ref[0]
    place_pairs(place, [own_mine], [own_theirs], kv, 0)
    place_pairs(place, rows[0::2], rows[1::2], qg, 0)
    heads, tokens, width = kv.shape[2:]
    scale = width ** (-0.5)
    factor = scale * LOG2E
    far = block_mask(reach, reach, tokens)
    for head in range(heads):
        for b in range(2):
            dk, dv = part[b, 0, head], part[b, 1, head]
            for a in range(2, b + reach + 1):
                q, g = qg[a - 2, 0, head], qg[a - 2, 1, head]
                source = stats[(a - 2) // 2]
                at = 2 * head + a % 2
                p, ds = score_grads(
                    kv[b, 0, head], kv[b, 1, head], q, g,
                    source[0, at : at + 1, :], source[1, at : at + 1, :],
                    far if a - b == reach else None, factor, scale,
                )
                dk = dk + dot(ds, q, NN)
                dv = dv + dot(p.astype(BF16), g, NN)
            out[b, 0, head], out[b, 1, head] = dk.astype(BF16), dv.astype(BF16)
    mine[...] = out[place]
    theirs[...] = out[1 - place]


def lane_scalars(values, count):
    lanes = lax.broadcasted_iota(jnp.int32, (1, 128), 1)
    row = jnp.zeros((1, 128), F32)
    for at in range(count):
        row = jnp.where(lanes == at, values[at], row)
    return row


def triangle(length):
    rows = lax.broadcasted_iota(jnp.int32, (length, length), 0)
    cols = lax.broadcasted_iota(jnp.int32, (length, length), 1)
    return rows, cols


def split_decay(rows):
    high = rows.astype(BF16).astype(F32)
    lanes = lax.broadcasted_iota(jnp.int32, rows.shape, 1)
    return jnp.where(lanes < 64, high, rows - high).astype(BF16)


def joined_decay(rows):
    rows = rows.astype(F32)
    return rows + pltpu.roll(rows, 64, 1)


def summary_body(rates_ref, dy_ref, dt_ref, bc_ref, base_ref, sent_ref, cum_ref, cumt_ref, wide):
    heads, tokens, width = dy_ref.shape
    wide[...] = jnp.zeros_like(wide)
    wide[:, :heads] = dt_ref[...]
    log_decay = wide[...] * lane_scalars(rates_ref, heads)
    rows, cols = triangle(tokens)
    cum = dot((cols <= rows).astype(F32), log_decay, NN, EXACT)
    cum_ref[...] = cum
    cumt = cum.T
    cumt_ref[...] = cumt[: cumt_ref.shape[0]]
    weights = jnp.exp(cum)
    last = jnp.exp(cumt[: cumt_ref.shape[0], tokens - 1 : tokens])
    bc = bc_ref[...].astype(F32)
    for head in range(heads):
        weighted = (bc * weights[:, head : head + 1]).astype(BF16)
        state = dot(weighted, dy_ref[head], TN)[NSTATE:]
        base_ref[head * NSTATE : (head + 1) * NSTATE] = state
        sent_ref[head * NSTATE : (head + 1) * NSTATE] = state.astype(BF16)
    decay = jnp.broadcast_to(last, (last.shape[0], width))
    base_ref[heads * NSTATE :] = decay
    sent_ref[heads * NSTATE :] = split_decay(decay)


def join_body(heads, first, base_ref, *refs):
    if first:
        got_ref, far_ref, sent_ref = refs
    else:
        far_old, got_ref, far_ref, sent_ref = refs
    tail = heads * NSTATE
    got_decay = joined_decay(got_ref[tail:])
    own = base_ref[tail:]
    if first:
        far_decay = got_decay
    else:
        old_decay = far_old[tail:]
        far_decay = old_decay * got_decay
    far_ref[tail:] = far_decay
    sent_ref[tail:] = split_decay(own * far_decay)
    for head in range(heads):
        rows = slice(head * NSTATE, (head + 1) * NSTATE)
        value = got_ref[rows].astype(F32)
        if not first:
            value = far_old[rows] + old_decay[head : head + 1] * value
        far_ref[rows] = value
        sent_ref[rows] = (base_ref[rows] + own[head : head + 1] * value).astype(BF16)


def scan_body(
    rates_ref, skips_ref, u_ref, dy_ref, dt_ref, bc_ref, start_ref, far_ref, cum_ref, cumt_ref,
    du_ref, steps_ref, gbc_ref, sums_ref, wide, columns, rows_one, rows_two,
):
    heads, tokens, width = u_ref.shape
    rates = lane_scalars(rates_ref, heads)
    wide[...] = jnp.zeros_like(wide)
    wide[:, :heads] = dt_ref[...]
    dt = wide[...]
    dtt = dt.T
    columns[...] = jnp.zeros_like(columns)
    rows_one[...] = jnp.zeros_like(rows_one)
    rows_two[...] = jnp.zeros_like(rows_two)
    cum, cumt = cum_ref[...], cumt_ref[...]
    bc = bc_ref[...]
    bct = bc.astype(F32).T
    bt, ct = bct[:NSTATE], bct[NSTATE:]
    c_only = bc[:, NSTATE:]
    b_only = bc[:, :NSTATE]
    inner = dot(b_only, c_only, NT)
    s_at, t_at = triangle(tokens)
    seen = s_at <= t_at
    inner = jnp.where(seen, inner, 0.0)
    last = cum[tokens - 1 : tokens]
    tail_all = jnp.exp(last - cum)
    weights_t = jnp.exp(cumt)
    tail_t = jnp.exp(cumt[:, tokens - 1 : tokens] - cumt)
    lanes = lax.broadcasted_iota(jnp.int32, (1, 128), 1)
    whole = jnp.zeros((1, 128), F32)
    skip_sum = jnp.zeros((1, 128), F32)
    pair_sum = None
    gb_t = jnp.zeros((NSTATE, tokens), F32)
    gc_t = jnp.zeros((NSTATE, tokens), F32)
    for head in range(heads):
        u, dy = u_ref[head], dy_ref[head]
        start = start_ref[head]
        far = far_ref[head * NSTATE : (head + 1) * NSTATE]
        far_low = far.astype(BF16)
        dt_col, dt_row = dt[:, head : head + 1], dtt[head : head + 1]
        spread = cumt[head : head + 1] - cum[:, head : head + 1]
        decay = jnp.where(seen, jnp.exp(jnp.where(seen, spread, 0.0)), 0.0)
        cross = dot(u, dy, NT)
        mixing = decay * inner
        product = mixing * cross
        weighted = decay * cross * dt_col
        pair_sum = weighted if pair_sum is None else pair_sum + weighted
        columns[:, head : head + 1] = jnp.sum(product, axis=1, keepdims=True)
        from_pairs = jnp.sum(product * dt_col, axis=0, keepdims=True)
        from_start = dot(start.astype(BF16), dy, NT) * weights_t[head : head + 1]
        gc_t = gc_t + from_start
        to_far = dot(far_low, u, NT) * tail_t[head : head + 1]
        gb_t = gb_t + to_far * dt_row
        rows_one[head : head + 1] = from_pairs + jnp.sum(from_start * ct, axis=0, keepdims=True)
        rows_two[head : head + 1] = jnp.sum(to_far * bt, axis=0, keepdims=True)
        driven = dot(mixing.astype(BF16), dy, NN)
        driven = driven + tail_all[:, head : head + 1] * dot(b_only, far_low, NN)
        dy_float = dy.astype(F32)
        du_ref[head] = (dt_col * driven + skips_ref[head] * dy_float).astype(BF16)
        own_whole = jnp.sum(jnp.sum(far * start, axis=0, keepdims=True), axis=1, keepdims=True)
        whole = jnp.where(lanes == head, own_whole, whole)
        own_skip = jnp.sum(
            jnp.sum(dy_float * u.astype(F32), axis=0, keepdims=True), axis=1, keepdims=True
        )
        skip_sum = jnp.where(lanes == head, own_skip, skip_sum)
    pair_low = pair_sum.astype(BF16)
    grad_b = dot(pair_low, c_only, NN) + gb_t.T
    grad_c = dot(pair_low, b_only, TN) + gc_t.T
    gbc_ref[:, :NSTATE] = grad_b.astype(BF16)
    gbc_ref[:, NSTATE:] = grad_c.astype(BF16)
    late = rows_two[...].T
    direct = columns[...] + late
    gathered = rows_one[...].T - dt * direct
    beyond = jnp.sum(dt * late, axis=0, keepdims=True) + jnp.exp(last) * whole
    grad_log = dot(seen.astype(F32), gathered, NN, EXACT) + beyond
    steps_ref[...] = (direct + rates * grad_log)[:, :heads]
    sums_ref[...] = jnp.zeros_like(sums_ref)
    sums_ref[0:1] = jnp.sum(dt * grad_log, axis=0, keepdims=True)
    sums_ref[1:2] = skip_sum


def shards(
    queries, key_vectors, values, out_grad, ssm_input, ssm_out_grad,
    step_sizes, decay_rates, skip_gains, bc_rows, saved_states,
):
    tokens, heads, width = queries.shape
    half = heads // 2
    reach = WINDOW // tokens
    hops = reach // 2
    at = lax.axis_index("seq")
    members = lax.axis_size("seq")
    place, pair = at % 2, at // 2
    where = jnp.stack([place, pair]).astype(jnp.int32)
    block = 2 * tokens * tokens * width

    sets = ssm_input.shape[1]
    held = -(-sets // 16) * 16
    u = jnp.transpose(ssm_input, (1, 0, 2))
    dy = jnp.transpose(ssm_out_grad, (1, 0, 2))
    packed = sets * NSTATE + held
    base, sent, cum, cumt = call(
        summary_body,
        [
            shape((packed, width), F32), shape((packed, width), BF16),
            shape((tokens, 128), F32), shape((held, tokens), F32),
        ],
        [decay_rates, dy, step_sizes, bc_rows],
        sets * block // 2, [pltpu.VMEM((tokens, 128), F32)], smem=1, name="summary",
    )

    def by_head(one, two):
        both = jnp.transpose(jnp.stack([one, two]), (0, 2, 1, 3))
        keep = lax.dynamic_slice_in_dim(both, place * half, half, 1)
        give = lax.dynamic_slice_in_dim(both, (1 - place) * half, half, 1)
        return keep, give

    kv_mine, kv_give = by_head(key_vectors, values)
    qg_mine, qg_give = by_head(queries, out_grad)
    kv_theirs = swapped(kv_give)
    qg_theirs = swapped(qg_give)
    keys = [(kv_mine, kv_theirs)]
    rows = [(qg_mine, qg_theirs)]
    for _ in range(hops):
        keys.insert(0, tuple(moved(v, 2) for v in keys[0]))
        rows.append(tuple(moved(v, -2) for v in rows[-1]))

    far = None
    step = 1
    while step < members:
        got = moved(sent, -step)
        ins = [base, got] if far is None else [base, far, got]
        far, sent = call(
            functools.partial(join_body, sets, far is None),
            [shape((packed, width), F32), shape((packed, width), BF16)],
            ins, packed * width * 4, name="join",
        )
        step *= 2
    du, grad_steps, gbc, sums = call(
        scan_body,
        [
            shape((sets, tokens, width), BF16), shape((tokens, sets), F32),
            shape((tokens, 2 * NSTATE), BF16), shape((8, 128), F32),
        ],
        [
            decay_rates, skip_gains, u, dy, step_sizes, bc_rows,
            saved_states.reshape(saved_states.shape[1:]), far, cum, cumt,
        ],
        sets * block * 4,
        [
            pltpu.VMEM((tokens, 128), F32), pltpu.VMEM((tokens, 128), F32),
            pltpu.VMEM((128, tokens), F32), pltpu.VMEM((128, tokens), F32),
        ],
        smem=2, name="scan",
    )
    grad_inputs = jnp.transpose(du, (1, 0, 2))
    gbc = lax.all_to_all(gbc, "head", 0, 0, tiled=True)
    grad_bc = jnp.sum(
        gbc.reshape(lax.axis_size("head"), -1, 2 * NSTATE).astype(F32), axis=0
    )
    spread = jnp.broadcast_to(sums[None], (members, *sums.shape))
    summed = jnp.sum(lax.all_to_all(spread, "seq", 0, 0, tiled=True), axis=0)
    grad_decay, grad_skip = summed[0, :sets], summed[1, :sets]

    flat = [v for both in keys for v in both]
    kv_space = pltpu.VMEM((2 * (hops + 1), 2, half, tokens, width), BF16)
    qg_space = pltpu.VMEM((2, 2, half, tokens, width), BF16)
    (stats,) = call(
        functools.partial(stats_body, reach),
        [shape((2, 2 * half, tokens), F32)],
        [where, *flat, qg_mine, qg_theirs],
        4 * (reach + 1) * half * block, [kv_space, qg_space], smem=1, name="stats",
    )
    later_stats = [moved(stats, -2 * (hop + 1)) for hop in range(hops)]
    dq_mine, dq_give, part = call(
        functools.partial(query_body, reach),
        [
            shape((half, tokens, width), BF16), shape((half, tokens, width), BF16),
            shape((2, 2, half, tokens, width), F32),
        ],
        [where, *flat, qg_mine, qg_theirs, stats],
        6 * (reach + 1) * half * block,
        [kv_space, qg_space, pltpu.VMEM((2, half, tokens, width), BF16)],
        smem=1, name="query",
    )
    dq_theirs = swapped(dq_give)
    later = [v for both in rows[1:] for v in both]
    dkv_mine, dkv_give = call(
        functools.partial(later_body, reach),
        [shape((2, half, tokens, width), BF16)] * 2,
        [where, kv_mine, kv_theirs, *later, *later_stats, part],
        8 * reach * half * block,
        [qg_space, pltpu.VMEM((2 * hops, 2, half, tokens, width), BF16), qg_space],
        smem=1, name="later",
    )
    dkv_theirs = swapped(dkv_give)

    def by_token(mine, theirs):
        first = jnp.where(place == 0, mine, theirs)
        second = jnp.where(place == 0, theirs, mine)
        return jnp.transpose(jnp.concatenate([first, second], axis=0), (1, 0, 2))

    query_grad = by_token(dq_mine, dq_theirs)
    key_grad = by_token(dkv_mine[0], dkv_theirs[0])
    value_grad = by_token(dkv_mine[1], dkv_theirs[1])
    return (
        query_grad, key_grad, value_grad, grad_inputs, grad_steps, grad_bc, grad_decay, grad_skip,
    )


def solution(mesh):
    wide = P("seq", "head", None)
    return jax.shard_map(
        shards,
        mesh=mesh,
        in_specs=(
            wide, wide, wide, wide, wide, wide, P("seq", "head"), P("head"), P("head"),
            P("seq", None), P("seq", "head", None, None),
        ),
        out_specs=(
            wide, wide, wide, wide, P("seq", "head"), P(("seq", "head"), None), P("head"), P("head"),
        ),
        check_vma=False,
    )
```

```python
import functools
import math

import jax
import jax.numpy as jnp
from jax import lax
from jax.experimental import pallas as pl
from jax.experimental.pallas import tpu as pltpu
from jax.sharding import PartitionSpec as P

NSTATE = 64
WINDOW = 1024
LOG2E = math.log2(math.e)
NEVER = -1e30
EXACT = lax.Precision.HIGHEST
F32 = jnp.float32
BF16 = jnp.bfloat16
VMEM_BYTES = 48 * 1024 * 1024


def dot(left, right, contract, precision=None):
    return lax.dot_general(
        left, right, (contract, ((), ())), precision=precision, preferred_element_type=F32
    )


NT = ((1,), (1,))
NN = ((1,), (0,))
TN = ((0,), (0,))


def moved(value, steps):
    count = lax.axis_size("seq")
    pairs = [(at, at + steps) for at in range(count) if 0 <= at + steps < count]
    return lax.ppermute(value, "seq", pairs)


def swapped(value):
    count = lax.axis_size("seq")
    return lax.ppermute(value, "seq", [(at, at ^ 1) for at in range(count)])


def after(value, *others):
    return lax.optimization_barrier((value, *others))[0]


def vmem(count):
    return [pl.BlockSpec(memory_space=pltpu.VMEM)] * count


def call(body, outs, ins, flops, scratch=(), smem=0, name=None):
    whole = sum(math.prod(v.shape) * v.dtype.itemsize for v in (*ins, *outs))
    specs = [pl.BlockSpec(memory_space=pltpu.SMEM)] * smem + vmem(len(ins) - smem)
    return pl.pallas_call(
        body,
        out_shape=outs,
        in_specs=specs,
        out_specs=vmem(len(outs)),
        scratch_shapes=list(scratch),
        compiler_params=pltpu.CompilerParams(vmem_limit_bytes=VMEM_BYTES),
        cost_estimate=pl.CostEstimate(flops=flops, bytes_accessed=whole, transcendentals=0),
        name=name,
    )(*ins)


def shape(dims, dtype):
    return jax.ShapeDtypeStruct(dims, dtype)


def block_mask(distance, reach, tokens):
    keys = lax.broadcasted_iota(jnp.int32, (tokens, tokens), 0)
    rows = lax.broadcasted_iota(jnp.int32, (tokens, tokens), 1)
    if distance == 0:
        return keys <= rows
    if distance == reach:
        return keys > rows
    return None


def dressed(value, factor, axis, masks, biases):
    count = len(masks)
    length = value.shape[axis] // count
    pieces = []
    for at in range(count):
        cut = slice(at * length, (at + 1) * length)
        piece = (value[cut] if axis == 0 else value[:, cut]) * factor
        if biases[at] is not None:
            piece = piece + biases[at]
        if masks[at] is not None:
            piece = jnp.where(masks[at], piece, NEVER)
        pieces.append(piece)
    return jnp.concatenate(pieces, axis=axis)


def band(ref, first, count, kind, head):
    rows = ref[first : first + count, kind, head]
    return rows.reshape(count * rows.shape[1], rows.shape[2])


def place_pairs(place, mine, theirs, target, first):
    for step in range(len(mine)):
        target[first + 2 * step + place] = mine[step][...]
        target[first + 2 * step + 1 - place] = theirs[step][...]


def online(kv, q, g, head, a, blocks, reach, factor, masks, biases, state):
    for j in blocks:
        s = dressed(
            dot(kv[j % 2 if kv.shape[0] == 2 else j, 0, head], q, NT), factor, 0,
            [masks[j - a]], [biases[j // 2]],
        )
        dp = dot(kv[j % 2 if kv.shape[0] == 2 else j, 1, head], g, NT)
        best = jnp.max(s, axis=0, keepdims=True)
        if state is not None:
            best = jnp.maximum(state[0], best)
        p = jnp.exp2(s - best)
        total = jnp.sum(p, axis=0, keepdims=True)
        delta = jnp.sum(p * dp, axis=0, keepdims=True)
        if state is not None:
            fade = jnp.exp2(state[0] - best)
            total, delta = state[1] * fade + total, state[2] * fade + delta
        state = (best, total, delta)
    return state


def early_body(reach, *refs):
    where_ref = refs[0]
    hops = reach // 2
    keys = refs[1 : 1 + 2 * hops]
    qg_mine, qg_theirs, out_ref, kv, qg = refs[1 + 2 * hops :]
    place, pair = where_ref[0], where_ref[1]
    place_pairs(place, keys[0::2], keys[1::2], kv, 2)
    place_pairs(place, [qg_mine], [qg_theirs], qg, 0)
    heads, tokens, width = kv.shape[2:]
    factor = width ** (-0.5) * LOG2E
    masks = [block_mask(reach - at, reach, tokens) for at in range(reach + 1)]
    biases = [jnp.where(pair >= hops - hop, 0.0, NEVER) for hop in range(hops)] + [None]
    for head in range(heads):
        for a in range(2):
            state = online(
                kv, qg[a, 0, head], qg[a, 1, head], head, a,
                range(a + reach, max(a, 2) - 1, -1), reach, factor, masks, biases, None,
            )
            at = 2 * head + a
            for kind in range(3):
                out_ref[kind, at : at + 1, :] = state[kind]


def late_body(reach, *refs):
    where_ref, far_mine, far_theirs, qg_mine, qg_theirs, early_ref, stats_ref, kv, qg = refs
    hops = reach // 2
    place, pair = where_ref[0], where_ref[1]
    place_pairs(place, [far_mine], [far_theirs], kv, 0)
    place_pairs(place, [qg_mine], [qg_theirs], qg, 0)
    heads, tokens, width = kv.shape[2:]
    factor = width ** (-0.5) * LOG2E
    masks = [block_mask(reach - at, reach, tokens) for at in range(reach + 1)]
    biases = [jnp.where(pair >= hops, 0.0, NEVER)]
    for head in range(heads):
        for a in range(2):
            at = 2 * head + a
            top, total, delta = online(
                kv, qg[a, 0, head], qg[a, 1, head], head, a, range(1, a - 1, -1), reach, factor,
                masks, biases, tuple(early_ref[kind, at : at + 1, :] for kind in range(3)),
            )
            stats_ref[0, at : at + 1, :] = top + jnp.log2(total)
            stats_ref[1, at : at + 1, :] = delta / total


def key_grads(key_block, value_block, q, g, lse, delta, masks, factor, scale):
    s = dressed(dot(key_block, q, NT), factor, 1, masks, [None] * len(masks))
    p = jnp.exp2(s - lse)
    dp = dot(value_block, g, NT)
    ds = (p * (dp - delta) * scale).astype(BF16)
    return dot(ds, q, NN), dot(p.astype(BF16), g, NN)


def stat_row(sources, kind, head, first, count):
    rows = [
        sources[a // 2][kind, 2 * head + a % 2 : 2 * head + a % 2 + 1, :]
        for a in range(first, first + count)
    ]
    return jnp.concatenate(rows, axis=1) if count > 1 else rows[0]


def query_body(reach, *refs):
    where_ref = refs[0]
    hops = reach // 2
    keys = refs[1 : 1 + 2 * (hops + 1)]
    qg_mine, qg_theirs, stats_ref, dq_mine, dq_theirs, part, kv, qg, dq, tall = refs[
        1 + 2 * (hops + 1) :
    ]
    place, pair = where_ref[0], where_ref[1]
    place_pairs(place, keys[0::2], keys[1::2], kv, 0)
    place_pairs(place, [qg_mine], [qg_theirs], qg, 0)
    heads, tokens, width = kv.shape[2:]
    scale = width ** (-0.5)
    factor = scale * LOG2E
    count = 2 * heads
    tall[...] = jnp.zeros_like(tall)
    tall[0:count] = stats_ref[0]
    tall[8 : 8 + count] = stats_ref[1]
    columns = tall[...].T
    rows = lax.broadcasted_iota(jnp.int32, (tokens, tokens), 0)
    cols = lax.broadcasted_iota(jnp.int32, (tokens, tokens), 1)
    flat = [cols > rows] + [None] * (reach - 1) + [cols <= rows]
    biases = [jnp.where(pair >= hops - hop, 0.0, NEVER) for hop in range(hops)] + [None]
    for head in range(heads):
        for a in range(2):
            at = 2 * head + a
            q, g = qg[a, 0, head], qg[a, 1, head]
            key_band = band(kv, a, reach + 1, 0, head)
            s = dressed(
                dot(q, key_band, NT), factor, 1, flat,
                [biases[j // 2] for j in range(a, a + reach + 1)],
            )
            p = jnp.exp2(s - columns[:, at : at + 1])
            dp = dot(g, band(kv, a, reach + 1, 1, head), NT)
            ds = (p * (dp - columns[:, 8 + at : 9 + at]) * scale).astype(BF16)
            dq[a, head] = dot(ds, key_band, NN).astype(BF16)
        for b in range(2):
            part[b, 0, head], part[b, 1, head] = key_grads(
                kv[b + reach, 0, head], kv[b + reach, 1, head],
                band(qg, b, 2 - b, 0, head), band(qg, b, 2 - b, 1, head),
                stat_row([stats_ref], 0, head, b, 2 - b), stat_row([stats_ref], 1, head, b, 2 - b),
                [block_mask(a - b, reach, tokens) for a in range(b, 2)], factor, scale,
            )
    dq_mine[...] = dq[place]
    dq_theirs[...] = dq[1 - place]


def later_body(reach, *refs):
    where_ref = refs[0]
    hops = reach // 2
    own_mine, own_theirs = refs[1:3]
    rows = refs[3 : 3 + 2 * hops]
    stats = refs[3 + 2 * hops : 3 + 3 * hops]
    part, mine, theirs, kv, qg, out = refs[3 + 3 * hops :]
    place = where_ref[0]
    place_pairs(place, [own_mine], [own_theirs], kv, 0)
    place_pairs(place, rows[0::2], rows[1::2], qg, 0)
    heads, tokens, width = kv.shape[2:]
    scale = width ** (-0.5)
    factor = scale * LOG2E
    for head in range(heads):
        for b in range(2):
            count = b + reach - 1
            dk, dv = key_grads(
                kv[b, 0, head], kv[b, 1, head],
                band(qg, 0, count, 0, head), band(qg, 0, count, 1, head),
                stat_row(stats, 0, head, 0, count), stat_row(stats, 1, head, 0, count),
                [block_mask(2 + at - b, reach, tokens) for at in range(count)], factor, scale,
            )
            out[b, 0, head] = (part[b, 0, head] + dk).astype(BF16)
            out[b, 1, head] = (part[b, 1, head] + dv).astype(BF16)
    mine[...] = out[place]
    theirs[...] = out[1 - place]


def lane_scalars(values, count):
    lanes = lax.broadcasted_iota(jnp.int32, (1, 128), 1)
    row = jnp.zeros((1, 128), F32)
    for at in range(count):
        row = jnp.where(lanes == at, values[at], row)
    return row


def triangle(length):
    rows = lax.broadcasted_iota(jnp.int32, (length, length), 0)
    cols = lax.broadcasted_iota(jnp.int32, (length, length), 1)
    return rows, cols


def split_decay(rows):
    high = rows.astype(BF16).astype(F32)
    lanes = lax.broadcasted_iota(jnp.int32, rows.shape, 1)
    return jnp.where(lanes < 64, high, rows - high).astype(BF16)


def joined_decay(rows):
    rows = rows.astype(F32)
    return rows + pltpu.roll(rows, 64, 1)


def summary_body(rates_ref, dy_ref, dt_ref, bc_ref, base_ref, sent_ref, cum_ref, cumt_ref, wide):
    heads, tokens, width = dy_ref.shape
    wide[...] = jnp.zeros_like(wide)
    wide[:, :heads] = dt_ref[...]
    log_decay = wide[...] * lane_scalars(rates_ref, heads)
    rows, cols = triangle(tokens)
    cum = dot((cols <= rows).astype(F32), log_decay, NN, EXACT)
    cum_ref[...] = cum
    cumt = cum.T
    cumt_ref[...] = cumt[: cumt_ref.shape[0]]
    weights = jnp.exp(cum)
    last = jnp.exp(cumt[: cumt_ref.shape[0], tokens - 1 : tokens])
    bc = bc_ref[...].astype(F32)
    for head in range(heads):
        weighted = (bc * weights[:, head : head + 1]).astype(BF16)
        state = dot(weighted, dy_ref[head], TN)[NSTATE:]
        base_ref[head * NSTATE : (head + 1) * NSTATE] = state
        sent_ref[head * NSTATE : (head + 1) * NSTATE] = state.astype(BF16)
    decay = jnp.broadcast_to(last, (last.shape[0], width))
    base_ref[heads * NSTATE :] = decay
    sent_ref[heads * NSTATE :] = split_decay(decay)


def join_body(heads, first, base_ref, *refs):
    if first:
        got_ref, far_ref, sent_ref = refs
    else:
        far_old, got_ref, far_ref, sent_ref = refs
    tail = heads * NSTATE
    got_decay = joined_decay(got_ref[tail:])
    own = base_ref[tail:]
    if first:
        far_decay = got_decay
    else:
        old_decay = far_old[tail:]
        far_decay = old_decay * got_decay
    far_ref[tail:] = far_decay
    sent_ref[tail:] = split_decay(own * far_decay)
    for head in range(heads):
        rows = slice(head * NSTATE, (head + 1) * NSTATE)
        value = got_ref[rows].astype(F32)
        if not first:
            value = far_old[rows] + old_decay[head : head + 1] * value
        far_ref[rows] = value
        sent_ref[rows] = (base_ref[rows] + own[head : head + 1] * value).astype(BF16)


def scan_body(
    rates_ref, skips_ref, u_ref, dy_ref, dt_ref, bc_ref, start_ref, far_ref, cum_ref, cumt_ref,
    du_ref, steps_ref, gbc_ref, sums_ref, wide, columns, rows_one, rows_two,
):
    heads, tokens, width = u_ref.shape
    rates = lane_scalars(rates_ref, heads)
    wide[...] = jnp.zeros_like(wide)
    wide[:, :heads] = dt_ref[...]
    dt = wide[...]
    dtt = dt.T
    columns[...] = jnp.zeros_like(columns)
    rows_one[...] = jnp.zeros_like(rows_one)
    rows_two[...] = jnp.zeros_like(rows_two)
    cum, cumt = cum_ref[...], cumt_ref[...]
    bc = bc_ref[...]
    bct = bc.astype(F32).T
    bt, ct = bct[:NSTATE], bct[NSTATE:]
    c_only = bc[:, NSTATE:]
    b_only = bc[:, :NSTATE]
    inner = dot(b_only, c_only, NT)
    s_at, t_at = triangle(tokens)
    seen = s_at <= t_at
    inner = jnp.where(seen, inner, 0.0)
    last = cum[tokens - 1 : tokens]
    tail_all = jnp.exp(last - cum)
    weights_t = jnp.exp(cumt)
    tail_t = jnp.exp(cumt[:, tokens - 1 : tokens] - cumt)
    lanes = lax.broadcasted_iota(jnp.int32, (1, 128), 1)
    whole = jnp.zeros((1, 128), F32)
    skip_sum = jnp.zeros((1, 128), F32)
    pair_sum = None
    gb_t = jnp.zeros((NSTATE, tokens), F32)
    gc_t = jnp.zeros((NSTATE, tokens), F32)
    for head in range(heads):
        u, dy = u_ref[head], dy_ref[head]
        start = start_ref[head]
        far = far_ref[head * NSTATE : (head + 1) * NSTATE]
        far_low = far.astype(BF16)
        dt_col, dt_row = dt[:, head : head + 1], dtt[head : head + 1]
        spread = cumt[head : head + 1] - cum[:, head : head + 1]
        decay = jnp.where(seen, jnp.exp(jnp.where(seen, spread, 0.0)), 0.0)
        cross = dot(u, dy, NT)
        mixing = decay * inner
        product = mixing * cross
        weighted = decay * cross * dt_col
        pair_sum = weighted if pair_sum is None else pair_sum + weighted
        columns[:, head : head + 1] = jnp.sum(product, axis=1, keepdims=True)
        from_pairs = jnp.sum(product * dt_col, axis=0, keepdims=True)
        from_start = dot(start.astype(BF16), dy, NT) * weights_t[head : head + 1]
        gc_t = gc_t + from_start
        to_far = dot(far_low, u, NT) * tail_t[head : head + 1]
        gb_t = gb_t + to_far * dt_row
        rows_one[head : head + 1] = from_pairs + jnp.sum(from_start * ct, axis=0, keepdims=True)
        rows_two[head : head + 1] = jnp.sum(to_far * bt, axis=0, keepdims=True)
        driven = dot(mixing.astype(BF16), dy, NN)
        driven = driven + tail_all[:, head : head + 1] * dot(b_only, far_low, NN)
        dy_float = dy.astype(F32)
        du_ref[head] = (dt_col * driven + skips_ref[head] * dy_float).astype(BF16)
        own_whole = jnp.sum(jnp.sum(far * start, axis=0, keepdims=True), axis=1, keepdims=True)
        whole = jnp.where(lanes == head, own_whole, whole)
        own_skip = jnp.sum(
            jnp.sum(dy_float * u.astype(F32), axis=0, keepdims=True), axis=1, keepdims=True
        )
        skip_sum = jnp.where(lanes == head, own_skip, skip_sum)
    pair_low = pair_sum.astype(BF16)
    grad_b = dot(pair_low, c_only, NN) + gb_t.T
    grad_c = dot(pair_low, b_only, TN) + gc_t.T
    gbc_ref[:, :NSTATE] = grad_b.astype(BF16)
    gbc_ref[:, NSTATE:] = grad_c.astype(BF16)
    late = rows_two[...].T
    direct = columns[...] + late
    gathered = rows_one[...].T - dt * direct
    beyond = jnp.sum(dt * late, axis=0, keepdims=True) + jnp.exp(last) * whole
    grad_log = dot(seen.astype(F32), gathered, NN, EXACT) + beyond
    steps_ref[...] = (direct + rates * grad_log)[:, :heads]
    sums_ref[...] = jnp.zeros_like(sums_ref)
    sums_ref[0:1] = jnp.sum(dt * grad_log, axis=0, keepdims=True)
    sums_ref[1:2] = skip_sum


def shards(
    queries, key_vectors, values, out_grad, ssm_input, ssm_out_grad,
    step_sizes, decay_rates, skip_gains, bc_rows, saved_states,
):
    tokens, heads, width = queries.shape
    half = heads // 2
    reach = WINDOW // tokens
    hops = reach // 2
    at = lax.axis_index("seq")
    members = lax.axis_size("seq")
    place, pair = at % 2, at // 2
    where = jnp.stack([place, pair]).astype(jnp.int32)
    block = 2 * tokens * tokens * width

    sets = ssm_input.shape[1]
    held = -(-sets // 16) * 16
    u = jnp.transpose(ssm_input, (1, 0, 2))
    dy = jnp.transpose(ssm_out_grad, (1, 0, 2))
    packed = sets * NSTATE + held
    base, sent, cum, cumt = call(
        summary_body,
        [
            shape((packed, width), F32), shape((packed, width), BF16),
            shape((tokens, 128), F32), shape((held, tokens), F32),
        ],
        [decay_rates, dy, step_sizes, bc_rows],
        sets * block // 2, [pltpu.VMEM((tokens, 128), F32)], smem=1, name="summary",
    )

    def by_head(one, two):
        both = jnp.transpose(jnp.stack([one, two]), (0, 2, 1, 3))
        keep = lax.dynamic_slice_in_dim(both, place * half, half, 1)
        give = lax.dynamic_slice_in_dim(both, (1 - place) * half, half, 1)
        return keep, give

    kv_mine, kv_give = by_head(key_vectors, values)
    qg_mine, qg_give = by_head(queries, out_grad)
    kv_theirs = swapped(kv_give)
    qg_theirs = swapped(qg_give)
    keys = [(kv_mine, kv_theirs)]
    for _ in range(hops):
        keys.insert(0, tuple(moved(v, 2) for v in keys[0]))

    gots = []
    far = None
    step = 1
    while step < members:
        got = moved(sent, -step)
        gots.append(got)
        if step == 2:
            base = after(base, keys[-2][1])
        if far is None:
            base = after(base, keys[-2][0])
        ins = [base, got] if far is None else [base, far, got]
        far, sent = call(
            functools.partial(join_body, sets, far is None),
            [shape((packed, width), F32), shape((packed, width), BF16)],
            ins, packed * width * 4, name="join",
        )
        step *= 2
    rows = [(qg_mine, qg_theirs)]
    source = (after(qg_mine, gots[0]), after(qg_theirs, gots[min(1, len(gots) - 1)]))
    for _ in range(hops):
        source = tuple(moved(v, -2) for v in source)
        rows.append(source)
    flat = [v for both in keys for v in both]
    kv_space = pltpu.VMEM((2 * (hops + 1), 2, half, tokens, width), BF16)
    qg_space = pltpu.VMEM((2, 2, half, tokens, width), BF16)
    (early,) = call(
        functools.partial(early_body, reach),
        [shape((3, 2 * half, tokens), F32)],
        [where, *flat[2:], qg_mine, qg_theirs],
        4 * (reach - 1) * half * block, [kv_space, qg_space], smem=1, name="early",
    )
    (stats,) = call(
        functools.partial(late_body, reach),
        [shape((2, 2 * half, tokens), F32)],
        [where, *flat[:2], qg_mine, qg_theirs, early],
        6 * half * block, [qg_space, qg_space], smem=1, name="late",
    )
    later_stats = [moved(stats, -2 * (hop + 1)) for hop in range(hops)]
    far = after(far, stats)
    du, grad_steps, gbc, sums = call(
        scan_body,
        [
            shape((sets, tokens, width), BF16), shape((tokens, sets), F32),
            shape((tokens, 2 * NSTATE), BF16), shape((8, 128), F32),
        ],
        [
            decay_rates, skip_gains, u, dy, step_sizes, bc_rows,
            saved_states.reshape(saved_states.shape[1:]), far, cum, cumt,
        ],
        sets * block * 4,
        [
            pltpu.VMEM((tokens, 128), F32), pltpu.VMEM((tokens, 128), F32),
            pltpu.VMEM((128, tokens), F32), pltpu.VMEM((128, tokens), F32),
        ],
        smem=2, name="scan",
    )
    grad_inputs = jnp.transpose(du, (1, 0, 2))
    gbc = lax.all_to_all(gbc, "head", 0, 0, tiled=True)
    grad_bc = jnp.sum(
        gbc.reshape(lax.axis_size("head"), -1, 2 * NSTATE).astype(F32), axis=0
    )

    dq_mine, dq_give, part = call(
        functools.partial(query_body, reach),
        [
            shape((half, tokens, width), BF16), shape((half, tokens, width), BF16),
            shape((2, 2, half, tokens, width), F32),
        ],
        [where, *flat, qg_mine, qg_theirs, stats],
        6 * (reach + 1) * half * block,
        [
            kv_space, qg_space, pltpu.VMEM((2, half, tokens, width), BF16),
            pltpu.VMEM((16, tokens), F32),
        ],
        smem=1, name="query",
    )
    dq_theirs = swapped(dq_give)
    later = [v for both in rows[1:] for v in both]
    dkv_mine, dkv_give = call(
        functools.partial(later_body, reach),
        [shape((2, half, tokens, width), BF16)] * 2,
        [where, kv_mine, kv_theirs, *later, *later_stats, part],
        8 * reach * half * block,
        [qg_space, pltpu.VMEM((2 * hops, 2, half, tokens, width), BF16), qg_space],
        smem=1, name="later",
    )
    dkv_theirs = swapped(dkv_give)

    sums = after(sums, dkv_give)
    spread = jnp.broadcast_to(sums[None], (members, *sums.shape))
    summed = jnp.sum(lax.all_to_all(spread, "seq", 0, 0, tiled=True), axis=0)
    grad_decay, grad_skip = summed[0, :sets], summed[1, :sets]

    def by_token(mine, theirs):
        first = jnp.where(place == 0, mine, theirs)
        second = jnp.where(place == 0, theirs, mine)
        return jnp.transpose(jnp.concatenate([first, second], axis=0), (1, 0, 2))

    query_grad = by_token(dq_mine, dq_theirs)
    key_grad = by_token(dkv_mine[0], dkv_theirs[0])
    value_grad = by_token(dkv_mine[1], dkv_theirs[1])
    return (
        query_grad, key_grad, value_grad, grad_inputs, grad_steps, grad_bc, grad_decay, grad_skip,
    )


def solution(mesh):
    wide = P("seq", "head", None)
    return jax.shard_map(
        shards,
        mesh=mesh,
        in_specs=(
            wide, wide, wide, wide, wide, wide, P("seq", "head"), P("head"), P("head"),
            P("seq", None), P("seq", "head", None, None),
        ),
        out_specs=(
            wide, wide, wide, wide, P("seq", "head"), P(("seq", "head"), None), P("head"), P("head"),
        ),
        check_vma=False,
    )
```

```python
import functools
import math

import jax
import jax.numpy as jnp
from jax import lax
from jax.experimental import pallas as pl
from jax.experimental.pallas import tpu as pltpu
from jax.sharding import PartitionSpec as P

NSTATE = 64
WINDOW = 1024
LOG2E = math.log2(math.e)
NEVER = -1e30
EXACT = lax.Precision.HIGHEST
F32 = jnp.float32
BF16 = jnp.bfloat16
VMEM_BYTES = 48 * 1024 * 1024


def dot(left, right, contract, precision=None):
    return lax.dot_general(
        left, right, (contract, ((), ())), precision=precision, preferred_element_type=F32
    )


NT = ((1,), (1,))
NN = ((1,), (0,))
TN = ((0,), (0,))


def moved(value, steps):
    count = lax.axis_size("seq")
    pairs = [(at, at + steps) for at in range(count) if 0 <= at + steps < count]
    return lax.ppermute(value, "seq", pairs)


def swapped(value):
    count = lax.axis_size("seq")
    return lax.ppermute(value, "seq", [(at, at ^ 1) for at in range(count)])


def after(value, *others):
    return lax.optimization_barrier((value, *others))[0]


def vmem(count):
    return [pl.BlockSpec(memory_space=pltpu.VMEM)] * count


def call(body, outs, ins, flops, scratch=(), smem=0, name=None):
    whole = sum(math.prod(v.shape) * v.dtype.itemsize for v in (*ins, *outs))
    specs = [pl.BlockSpec(memory_space=pltpu.SMEM)] * smem + vmem(len(ins) - smem)
    return pl.pallas_call(
        body,
        out_shape=outs,
        in_specs=specs,
        out_specs=vmem(len(outs)),
        scratch_shapes=list(scratch),
        compiler_params=pltpu.CompilerParams(vmem_limit_bytes=VMEM_BYTES),
        cost_estimate=pl.CostEstimate(flops=flops, bytes_accessed=whole, transcendentals=0),
        name=name,
    )(*ins)


def shape(dims, dtype):
    return jax.ShapeDtypeStruct(dims, dtype)


def block_mask(distance, reach, tokens):
    keys = lax.broadcasted_iota(jnp.int32, (tokens, tokens), 0)
    rows = lax.broadcasted_iota(jnp.int32, (tokens, tokens), 1)
    if distance == 0:
        return keys <= rows
    if distance == reach:
        return keys > rows
    return None


def dressed(value, factor, axis, masks, biases):
    count = len(masks)
    length = value.shape[axis] // count
    pieces = []
    for at in range(count):
        cut = slice(at * length, (at + 1) * length)
        piece = (value[cut] if axis == 0 else value[:, cut]) * factor
        if biases[at] is not None:
            piece = piece + biases[at]
        if masks[at] is not None:
            piece = jnp.where(masks[at], piece, NEVER)
        pieces.append(piece)
    return jnp.concatenate(pieces, axis=axis)


def band(ref, first, count, kind, head):
    rows = ref[first : first + count, kind, head]
    return rows.reshape(count * rows.shape[1], rows.shape[2])


def place_pairs(place, mine, theirs, target, first):
    for step in range(len(mine)):
        target[first + 2 * step + place] = mine[step][...]
        target[first + 2 * step + 1 - place] = theirs[step][...]


def online(kv, q, g, head, a, blocks, reach, factor, masks, biases, state):
    for j in blocks:
        s = dressed(
            dot(kv[j % 2 if kv.shape[0] == 2 else j, 0, head], q, NT), factor, 0,
            [masks[j - a]], [biases[j // 2]],
        )
        dp = dot(kv[j % 2 if kv.shape[0] == 2 else j, 1, head], g, NT)
        best = jnp.max(s, axis=0, keepdims=True)
        if state is not None:
            best = jnp.maximum(state[0], best)
        p = jnp.exp2(s - best)
        total = jnp.sum(p, axis=0, keepdims=True)
        delta = jnp.sum(p * dp, axis=0, keepdims=True)
        if state is not None:
            fade = jnp.exp2(state[0] - best)
            total, delta = state[1] * fade + total, state[2] * fade + delta
        state = (best, total, delta)
    return state


def early_body(reach, *refs):
    where_ref = refs[0]
    hops = reach // 2
    keys = refs[1 : 1 + 2 * hops]
    qg_mine, qg_theirs, out_ref, kv, qg = refs[1 + 2 * hops :]
    place, pair = where_ref[0], where_ref[1]
    place_pairs(place, keys[0::2], keys[1::2], kv, 2)
    place_pairs(place, [qg_mine], [qg_theirs], qg, 0)
    heads, tokens, width = kv.shape[2:]
    factor = width ** (-0.5) * LOG2E
    masks = [block_mask(reach - at, reach, tokens) for at in range(reach + 1)]
    biases = [jnp.where(pair >= hops - hop, 0.0, NEVER) for hop in range(hops)] + [None]
    for head in range(heads):
        for a in range(2):
            state = online(
                kv, qg[a, 0, head], qg[a, 1, head], head, a,
                range(a + reach, max(a, 2) - 1, -1), reach, factor, masks, biases, None,
            )
            at = 2 * head + a
            for kind in range(3):
                out_ref[kind, at : at + 1, :] = state[kind]


def late_body(reach, *refs):
    where_ref, far_mine, far_theirs, qg_mine, qg_theirs, early_ref, stats_ref, kv, qg = refs
    hops = reach // 2
    place, pair = where_ref[0], where_ref[1]
    place_pairs(place, [far_mine], [far_theirs], kv, 0)
    place_pairs(place, [qg_mine], [qg_theirs], qg, 0)
    heads, tokens, width = kv.shape[2:]
    factor = width ** (-0.5) * LOG2E
    masks = [block_mask(reach - at, reach, tokens) for at in range(reach + 1)]
    biases = [jnp.where(pair >= hops, 0.0, NEVER)]
    for head in range(heads):
        for a in range(2):
            at = 2 * head + a
            top, total, delta = online(
                kv, qg[a, 0, head], qg[a, 1, head], head, a, range(1, a - 1, -1), reach, factor,
                masks, biases, tuple(early_ref[kind, at : at + 1, :] for kind in range(3)),
            )
            stats_ref[0, at : at + 1, :] = top + jnp.log2(total)
            stats_ref[1, at : at + 1, :] = delta / total


def key_grads(key_block, value_block, q, g, lse, delta, masks, factor, scale):
    s = dressed(dot(key_block, q, NT), factor, 1, masks, [None] * len(masks))
    p = jnp.exp2(s - lse)
    dp = dot(value_block, g, NT)
    ds = (p * (dp - delta) * scale).astype(BF16)
    return dot(ds, q, NN), dot(p.astype(BF16), g, NN)


def stat_row(sources, kind, head, first, count):
    rows = [
        sources[a // 2][kind, 2 * head + a % 2 : 2 * head + a % 2 + 1, :]
        for a in range(first, first + count)
    ]
    return jnp.concatenate(rows, axis=1) if count > 1 else rows[0]


def query_body(reach, *refs):
    where_ref = refs[0]
    hops = reach // 2
    keys = refs[1 : 1 + 2 * (hops + 1)]
    qg_mine, qg_theirs, stats_ref, dq_mine, dq_theirs, part, kv, qg, dq, tall = refs[
        1 + 2 * (hops + 1) :
    ]
    place, pair = where_ref[0], where_ref[1]
    place_pairs(place, keys[0::2], keys[1::2], kv, 0)
    place_pairs(place, [qg_mine], [qg_theirs], qg, 0)
    heads, tokens, width = kv.shape[2:]
    scale = width ** (-0.5)
    factor = scale * LOG2E
    count = 2 * heads
    tall[...] = jnp.zeros_like(tall)
    tall[0:count] = stats_ref[0]
    tall[8 : 8 + count] = stats_ref[1]
    columns = tall[...].T
    rows = lax.broadcasted_iota(jnp.int32, (tokens, tokens), 0)
    cols = lax.broadcasted_iota(jnp.int32, (tokens, tokens), 1)
    flat = [cols > rows] + [None] * (reach - 1) + [cols <= rows]
    biases = [jnp.where(pair >= hops - hop, 0.0, NEVER) for hop in range(hops)] + [None]
    for head in range(heads):
        for a in range(2):
            at = 2 * head + a
            q, g = qg[a, 0, head], qg[a, 1, head]
            key_band = band(kv, a, reach + 1, 0, head)
            s = dressed(
                dot(q, key_band, NT), factor, 1, flat,
                [biases[j // 2] for j in range(a, a + reach + 1)],
            )
            p = jnp.exp2(s - columns[:, at : at + 1])
            dp = dot(g, band(kv, a, reach + 1, 1, head), NT)
            ds = (p * (dp - columns[:, 8 + at : 9 + at]) * scale).astype(BF16)
            dq[a, head] = dot(ds, key_band, NN).astype(BF16)
        for b in range(2):
            part[b, 0, head], part[b, 1, head] = key_grads(
                kv[b + reach, 0, head], kv[b + reach, 1, head],
                band(qg, b, 2 - b, 0, head), band(qg, b, 2 - b, 1, head),
                stat_row([stats_ref], 0, head, b, 2 - b), stat_row([stats_ref], 1, head, b, 2 - b),
                [block_mask(a - b, reach, tokens) for a in range(b, 2)], factor, scale,
            )
    dq_mine[...] = dq[place]
    dq_theirs[...] = dq[1 - place]


def later_body(reach, *refs):
    where_ref = refs[0]
    hops = reach // 2
    own_mine, own_theirs = refs[1:3]
    rows = refs[3 : 3 + 2 * hops]
    stats = refs[3 + 2 * hops : 3 + 3 * hops]
    part, mine, theirs, kv, qg, out = refs[3 + 3 * hops :]
    place = where_ref[0]
    place_pairs(place, [own_mine], [own_theirs], kv, 0)
    place_pairs(place, rows[0::2], rows[1::2], qg, 0)
    heads, tokens, width = kv.shape[2:]
    scale = width ** (-0.5)
    factor = scale * LOG2E
    for head in range(heads):
        for b in range(2):
            count = b + reach - 1
            dk, dv = key_grads(
                kv[b, 0, head], kv[b, 1, head],
                band(qg, 0, count, 0, head), band(qg, 0, count, 1, head),
                stat_row(stats, 0, head, 0, count), stat_row(stats, 1, head, 0, count),
                [block_mask(2 + at - b, reach, tokens) for at in range(count)], factor, scale,
            )
            out[b, 0, head] = (part[b, 0, head] + dk).astype(BF16)
            out[b, 1, head] = (part[b, 1, head] + dv).astype(BF16)
    mine[...] = out[place]
    theirs[...] = out[1 - place]


def lane_scalars(values, count):
    lanes = lax.broadcasted_iota(jnp.int32, (1, 128), 1)
    row = jnp.zeros((1, 128), F32)
    for at in range(count):
        row = jnp.where(lanes == at, values[at], row)
    return row


def triangle(length):
    rows = lax.broadcasted_iota(jnp.int32, (length, length), 0)
    cols = lax.broadcasted_iota(jnp.int32, (length, length), 1)
    return rows, cols


def split_decay(rows):
    high = rows.astype(BF16).astype(F32)
    lanes = lax.broadcasted_iota(jnp.int32, rows.shape, 1)
    return jnp.where(lanes < 64, high, rows - high).astype(BF16)


def joined_decay(rows):
    rows = rows.astype(F32)
    return rows + pltpu.roll(rows, 64, 1)


def summary_body(rates_ref, dy_ref, dt_ref, bc_ref, base_ref, sent_ref, cum_ref, cumt_ref, wide):
    heads, tokens, width = dy_ref.shape
    wide[...] = jnp.zeros_like(wide)
    wide[:, :heads] = dt_ref[...]
    log_decay = wide[...] * lane_scalars(rates_ref, heads)
    rows, cols = triangle(tokens)
    cum = dot((cols <= rows).astype(F32), log_decay, NN, EXACT)
    cum_ref[...] = cum
    cumt = cum.T
    cumt_ref[...] = cumt[: cumt_ref.shape[0]]
    weights = jnp.exp(cum)
    last = jnp.exp(cumt[: cumt_ref.shape[0], tokens - 1 : tokens])
    bc = bc_ref[...].astype(F32)
    for head in range(heads):
        weighted = (bc * weights[:, head : head + 1]).astype(BF16)
        state = dot(weighted, dy_ref[head], TN)[NSTATE:]
        base_ref[head * NSTATE : (head + 1) * NSTATE] = state
        sent_ref[head * NSTATE : (head + 1) * NSTATE] = state.astype(BF16)
    decay = jnp.broadcast_to(last, (last.shape[0], width))
    base_ref[heads * NSTATE :] = decay
    sent_ref[heads * NSTATE :] = split_decay(decay)


def join_body(heads, first, base_ref, *refs):
    if first:
        got_ref, far_ref, sent_ref = refs
    else:
        far_old, got_ref, far_ref, sent_ref = refs
    tail = heads * NSTATE
    got_decay = joined_decay(got_ref[tail:])
    own = base_ref[tail:]
    if first:
        far_decay = got_decay
    else:
        old_decay = far_old[tail:]
        far_decay = old_decay * got_decay
    far_ref[tail:] = far_decay
    sent_ref[tail:] = split_decay(own * far_decay)
    for head in range(heads):
        rows = slice(head * NSTATE, (head + 1) * NSTATE)
        value = got_ref[rows].astype(F32)
        if not first:
            value = far_old[rows] + old_decay[head : head + 1] * value
        far_ref[rows] = value
        sent_ref[rows] = (base_ref[rows] + own[head : head + 1] * value).astype(BF16)


def scan_body(
    rates_ref, skips_ref, u_ref, dy_ref, dt_ref, bc_ref, start_ref, far_ref, cum_ref, cumt_ref,
    du_ref, steps_ref, gbc_ref, sums_ref, wide, columns, rows_one, rows_two,
):
    heads, tokens, width = u_ref.shape
    rates = lane_scalars(rates_ref, heads)
    wide[...] = jnp.zeros_like(wide)
    wide[:, :heads] = dt_ref[...]
    dt = wide[...]
    dtt = dt.T
    columns[...] = jnp.zeros_like(columns)
    rows_one[...] = jnp.zeros_like(rows_one)
    rows_two[...] = jnp.zeros_like(rows_two)
    cum, cumt = cum_ref[...], cumt_ref[...]
    bc = bc_ref[...]
    bct = bc.astype(F32).T
    bt, ct = bct[:NSTATE], bct[NSTATE:]
    c_only = bc[:, NSTATE:]
    b_only = bc[:, :NSTATE]
    inner = dot(b_only, c_only, NT)
    s_at, t_at = triangle(tokens)
    seen = s_at <= t_at
    inner = jnp.where(seen, inner, 0.0)
    last = cum[tokens - 1 : tokens]
    tail_all = jnp.exp(last - cum)
    weights_t = jnp.exp(cumt)
    tail_t = jnp.exp(cumt[:, tokens - 1 : tokens] - cumt)
    lanes = lax.broadcasted_iota(jnp.int32, (1, 128), 1)
    whole = jnp.zeros((1, 128), F32)
    skip_sum = jnp.zeros((1, 128), F32)
    pair_sum = None
    gb_t = jnp.zeros((NSTATE, tokens), F32)
    gc_t = jnp.zeros((NSTATE, tokens), F32)
    for head in range(heads):
        u, dy = u_ref[head], dy_ref[head]
        start = start_ref[head]
        far = far_ref[head * NSTATE : (head + 1) * NSTATE]
        far_low = far.astype(BF16)
        dt_col, dt_row = dt[:, head : head + 1], dtt[head : head + 1]
        spread = cumt[head : head + 1] - cum[:, head : head + 1]
        decay = jnp.where(seen, jnp.exp(jnp.where(seen, spread, 0.0)), 0.0)
        cross = dot(u, dy, NT)
        mixing = decay * inner
        product = mixing * cross
        weighted = decay * cross * dt_col
        pair_sum = weighted if pair_sum is None else pair_sum + weighted
        columns[:, head : head + 1] = jnp.sum(product, axis=1, keepdims=True)
        from_pairs = jnp.sum(product * dt_col, axis=0, keepdims=True)
        from_start = dot(start.astype(BF16), dy, NT) * weights_t[head : head + 1]
        gc_t = gc_t + from_start
        to_far = dot(far_low, u, NT) * tail_t[head : head + 1]
        gb_t = gb_t + to_far * dt_row
        rows_one[head : head + 1] = from_pairs + jnp.sum(from_start * ct, axis=0, keepdims=True)
        rows_two[head : head + 1] = jnp.sum(to_far * bt, axis=0, keepdims=True)
        driven = dot(mixing.astype(BF16), dy, NN)
        driven = driven + tail_all[:, head : head + 1] * dot(b_only, far_low, NN)
        dy_float = dy.astype(F32)
        du_ref[head] = (dt_col * driven + skips_ref[head] * dy_float).astype(BF16)
        own_whole = jnp.sum(jnp.sum(far * start, axis=0, keepdims=True), axis=1, keepdims=True)
        whole = jnp.where(lanes == head, own_whole, whole)
        own_skip = jnp.sum(
            jnp.sum(dy_float * u.astype(F32), axis=0, keepdims=True), axis=1, keepdims=True
        )
        skip_sum = jnp.where(lanes == head, own_skip, skip_sum)
    pair_low = pair_sum.astype(BF16)
    grad_b = dot(pair_low, c_only, NN) + gb_t.T
    grad_c = dot(pair_low, b_only, TN) + gc_t.T
    gbc_ref[:, :NSTATE] = grad_b.astype(BF16)
    gbc_ref[:, NSTATE:] = grad_c.astype(BF16)
    late = rows_two[...].T
    direct = columns[...] + late
    gathered = rows_one[...].T - dt * direct
    beyond = jnp.sum(dt * late, axis=0, keepdims=True) + jnp.exp(last) * whole
    grad_log = dot(seen.astype(F32), gathered, NN, EXACT) + beyond
    steps_ref[...] = (direct + rates * grad_log)[:, :heads]
    sums_ref[...] = jnp.zeros_like(sums_ref)
    sums_ref[0:1] = jnp.sum(dt * grad_log, axis=0, keepdims=True)
    sums_ref[1:2] = skip_sum


def shards(
    queries, key_vectors, values, out_grad, ssm_input, ssm_out_grad,
    step_sizes, decay_rates, skip_gains, bc_rows, saved_states,
):
    tokens, heads, width = queries.shape
    half = heads // 2
    reach = WINDOW // tokens
    hops = reach // 2
    at = lax.axis_index("seq")
    members = lax.axis_size("seq")
    place, pair = at % 2, at // 2
    where = jnp.stack([place, pair]).astype(jnp.int32)
    block = 2 * tokens * tokens * width

    sets = ssm_input.shape[1]
    held = -(-sets // 16) * 16
    u = jnp.transpose(ssm_input, (1, 0, 2))
    dy = jnp.transpose(ssm_out_grad, (1, 0, 2))
    packed = sets * NSTATE + held
    base, sent, cum, cumt = call(
        summary_body,
        [
            shape((packed, width), F32), shape((packed, width), BF16),
            shape((tokens, 128), F32), shape((held, tokens), F32),
        ],
        [decay_rates, dy, step_sizes, bc_rows],
        sets * block // 2, [pltpu.VMEM((tokens, 128), F32)], smem=1, name="summary",
    )

    def by_head(one, two):
        both = jnp.transpose(jnp.stack([one, two]), (0, 2, 1, 3))
        keep = lax.dynamic_slice_in_dim(both, place * half, half, 1)
        give = lax.dynamic_slice_in_dim(both, (1 - place) * half, half, 1)
        return keep, give

    kv_mine, kv_give = by_head(key_vectors, values)
    qg_mine, qg_give = by_head(queries, out_grad)
    kv_theirs = swapped(kv_give)
    qg_theirs = swapped(qg_give)
    keys = [(kv_mine, kv_theirs)]
    for _ in range(hops):
        keys.insert(0, tuple(moved(v, 2) for v in keys[0]))

    rows = [(qg_mine, qg_theirs), (moved(qg_mine, -2), moved(qg_theirs, -2))]
    gots = []
    far = None
    step = 1
    while step < members:
        got = moved(sent, -step)
        gots.append(got)
        if step == 2:
            base = after(base, keys[-2][1])
        if far is None:
            base = after(base, keys[-2][0], rows[1][0])
        ins = [base, got] if far is None else [base, far, got]
        far, sent = call(
            functools.partial(join_body, sets, far is None),
            [shape((packed, width), F32), shape((packed, width), BF16)],
            ins, packed * width * 4, name="join",
        )
        step *= 2
    flat = [v for both in keys for v in both]
    kv_space = pltpu.VMEM((2 * (hops + 1), 2, half, tokens, width), BF16)
    qg_space = pltpu.VMEM((2, 2, half, tokens, width), BF16)
    (early,) = call(
        functools.partial(early_body, reach),
        [shape((3, 2 * half, tokens), F32)],
        [where, *flat[2:], qg_mine, qg_theirs],
        4 * (reach - 1) * half * block, [kv_space, qg_space], smem=1, name="early",
    )
    (stats,) = call(
        functools.partial(late_body, reach),
        [shape((2, 2 * half, tokens), F32)],
        [where, *flat[:2], qg_mine, qg_theirs, early],
        6 * half * block, [qg_space, qg_space], smem=1, name="late",
    )
    later_stats = [moved(stats, -2 * (hop + 1)) for hop in range(hops)]
    far = after(far, stats)
    du, grad_steps, gbc, sums = call(
        scan_body,
        [
            shape((sets, tokens, width), BF16), shape((tokens, sets), F32),
            shape((tokens, 2 * NSTATE), BF16), shape((8, 128), F32),
        ],
        [
            decay_rates, skip_gains, u, dy, step_sizes, bc_rows,
            saved_states.reshape(saved_states.shape[1:]), far, cum, cumt,
        ],
        sets * block * 4,
        [
            pltpu.VMEM((tokens, 128), F32), pltpu.VMEM((tokens, 128), F32),
            pltpu.VMEM((128, tokens), F32), pltpu.VMEM((128, tokens), F32),
        ],
        smem=2, name="scan",
    )
    grad_inputs = jnp.transpose(du, (1, 0, 2))
    gbc = lax.all_to_all(gbc, "head", 0, 0, tiled=True)
    grad_bc = jnp.sum(
        gbc.reshape(lax.axis_size("head"), -1, 2 * NSTATE).astype(F32), axis=0
    )

    dq_mine, dq_give, part = call(
        functools.partial(query_body, reach),
        [
            shape((half, tokens, width), BF16), shape((half, tokens, width), BF16),
            shape((2, 2, half, tokens, width), F32),
        ],
        [where, *flat, qg_mine, qg_theirs, stats],
        6 * (reach + 1) * half * block,
        [
            kv_space, qg_space, pltpu.VMEM((2, half, tokens, width), BF16),
            pltpu.VMEM((16, tokens), F32),
        ],
        smem=1, name="query",
    )
    dq_theirs = swapped(dq_give)
    for hop in range(1, hops):
        one, two = rows[-1]
        rows.append((moved(after(one, early), -2), moved(after(two, early), -2)))
    later = [v for both in rows[1:] for v in both]
    pair_sums = swapped(sums)
    dkv_mine, dkv_give = call(
        functools.partial(later_body, reach),
        [shape((2, half, tokens, width), BF16)] * 2,
        [where, kv_mine, kv_theirs, *later, *later_stats, part],
        8 * reach * half * block,
        [qg_space, pltpu.VMEM((2 * hops, 2, half, tokens, width), BF16), qg_space],
        smem=1, name="later",
    )
    dkv_theirs = swapped(dkv_give)

    sums = after(sums + pair_sums, dkv_give)
    pairs = members // 2
    spread = jnp.broadcast_to(sums[None], (pairs, *sums.shape))
    lines = [[2 * at + one for at in range(pairs)] for one in range(2)]
    summed = jnp.sum(
        lax.all_to_all(spread, "seq", 0, 0, axis_index_groups=lines, tiled=True), axis=0
    )
    grad_decay, grad_skip = summed[0, :sets], summed[1, :sets]

    def by_token(mine, theirs):
        first = jnp.where(place == 0, mine, theirs)
        second = jnp.where(place == 0, theirs, mine)
        return jnp.transpose(jnp.concatenate([first, second], axis=0), (1, 0, 2))

    query_grad = by_token(dq_mine, dq_theirs)
    key_grad = by_token(dkv_mine[0], dkv_theirs[0])
    value_grad = by_token(dkv_mine[1], dkv_theirs[1])
    return (
        query_grad, key_grad, value_grad, grad_inputs, grad_steps, grad_bc, grad_decay, grad_skip,
    )


def solution(mesh):
    wide = P("seq", "head", None)
    return jax.shard_map(
        shards,
        mesh=mesh,
        in_specs=(
            wide, wide, wide, wide, wide, wide, P("seq", "head"), P("head"), P("head"),
            P("seq", None), P("seq", "head", None, None),
        ),
        out_specs=(
            wide, wide, wide, wide, P("seq", "head"), P(("seq", "head"), None), P("head"), P("head"),
        ),
        check_vma=False,
    )
```

```python
import functools
import math

import jax
import jax.numpy as jnp
from jax import lax
from jax.experimental import pallas as pl
from jax.experimental.pallas import tpu as pltpu
from jax.sharding import PartitionSpec as P

NSTATE = 64
WINDOW = 1024
LOG2E = math.log2(math.e)
NEVER = -1e30
EXACT = lax.Precision.HIGHEST
F32 = jnp.float32
BF16 = jnp.bfloat16
VMEM_BYTES = 48 * 1024 * 1024


def dot(left, right, contract, precision=None):
    return lax.dot_general(
        left, right, (contract, ((), ())), precision=precision, preferred_element_type=F32
    )


NT = ((1,), (1,))
NN = ((1,), (0,))
TN = ((0,), (0,))


def moved(value, steps):
    count = lax.axis_size("seq")
    pairs = [(at, at + steps) for at in range(count) if 0 <= at + steps < count]
    return lax.ppermute(value, "seq", pairs)


def swapped(value):
    count = lax.axis_size("seq")
    return lax.ppermute(value, "seq", [(at, at ^ 1) for at in range(count)])


def after(value, *others):
    return lax.optimization_barrier((value, *others))[0]


def vmem(count):
    return [pl.BlockSpec(memory_space=pltpu.VMEM)] * count


def call(body, outs, ins, flops, scratch=(), smem=0, name=None):
    whole = sum(math.prod(v.shape) * v.dtype.itemsize for v in (*ins, *outs))
    specs = [pl.BlockSpec(memory_space=pltpu.SMEM)] * smem + vmem(len(ins) - smem)
    return pl.pallas_call(
        body,
        out_shape=outs,
        in_specs=specs,
        out_specs=vmem(len(outs)),
        scratch_shapes=list(scratch),
        compiler_params=pltpu.CompilerParams(vmem_limit_bytes=VMEM_BYTES),
        cost_estimate=pl.CostEstimate(flops=flops, bytes_accessed=whole, transcendentals=0),
        name=name,
    )(*ins)


def shape(dims, dtype):
    return jax.ShapeDtypeStruct(dims, dtype)


def block_mask(distance, reach, tokens):
    keys = lax.broadcasted_iota(jnp.int32, (tokens, tokens), 0)
    rows = lax.broadcasted_iota(jnp.int32, (tokens, tokens), 1)
    if distance == 0:
        return keys <= rows
    if distance == reach:
        return keys > rows
    return None


def dressed(value, factor, axis, masks, biases):
    count = len(masks)
    length = value.shape[axis] // count
    pieces = []
    for at in range(count):
        cut = slice(at * length, (at + 1) * length)
        piece = (value[cut] if axis == 0 else value[:, cut]) * factor
        if biases[at] is not None:
            piece = piece + biases[at]
        if masks[at] is not None:
            piece = jnp.where(masks[at], piece, NEVER)
        pieces.append(piece)
    return jnp.concatenate(pieces, axis=axis)


def band(ref, first, count, kind, head):
    rows = ref[first : first + count, kind, head]
    return rows.reshape(count * rows.shape[1], rows.shape[2])


def place_pairs(place, mine, theirs, target, first):
    for step in range(len(mine)):
        target[first + 2 * step + place] = mine[step][...]
        target[first + 2 * step + 1 - place] = theirs[step][...]


def online(kv, q, g, head, a, blocks, reach, factor, masks, biases, state):
    for j in blocks:
        s = dressed(
            dot(kv[j % 2 if kv.shape[0] == 2 else j, 0, head], q, NT), factor, 0,
            [masks[j - a]], [biases[j // 2]],
        )
        dp = dot(kv[j % 2 if kv.shape[0] == 2 else j, 1, head], g, NT)
        best = jnp.max(s, axis=0, keepdims=True)
        if state is not None:
            best = jnp.maximum(state[0], best)
        p = jnp.exp2(s - best)
        total = jnp.sum(p, axis=0, keepdims=True)
        delta = jnp.sum(p * dp, axis=0, keepdims=True)
        if state is not None:
            fade = jnp.exp2(state[0] - best)
            total, delta = state[1] * fade + total, state[2] * fade + delta
        state = (best, total, delta)
    return state


def early_body(reach, *refs):
    where_ref = refs[0]
    hops = reach // 2
    keys = refs[1 : 1 + 2 * hops]
    qg_mine, qg_theirs, out_ref, kv, qg = refs[1 + 2 * hops :]
    place, pair = where_ref[0], where_ref[1]
    place_pairs(place, keys[0::2], keys[1::2], kv, 2)
    place_pairs(place, [qg_mine], [qg_theirs], qg, 0)
    heads, tokens, width = kv.shape[2:]
    factor = width ** (-0.5) * LOG2E
    masks = [block_mask(reach - at, reach, tokens) for at in range(reach + 1)]
    biases = [jnp.where(pair >= hops - hop, 0.0, NEVER) for hop in range(hops)] + [None]
    for head in range(heads):
        for a in range(2):
            state = online(
                kv, qg[a, 0, head], qg[a, 1, head], head, a,
                range(a + reach, max(a, 2) - 1, -1), reach, factor, masks, biases, None,
            )
            at = 2 * head + a
            for kind in range(3):
                out_ref[kind, at : at + 1, :] = state[kind]


def late_body(reach, *refs):
    where_ref, far_mine, far_theirs, qg_mine, qg_theirs, early_ref, stats_ref, kv, qg = refs
    hops = reach // 2
    place, pair = where_ref[0], where_ref[1]
    place_pairs(place, [far_mine], [far_theirs], kv, 0)
    place_pairs(place, [qg_mine], [qg_theirs], qg, 0)
    heads, tokens, width = kv.shape[2:]
    factor = width ** (-0.5) * LOG2E
    masks = [block_mask(reach - at, reach, tokens) for at in range(reach + 1)]
    biases = [jnp.where(pair >= hops, 0.0, NEVER)]
    for head in range(heads):
        for a in range(2):
            at = 2 * head + a
            top, total, delta = online(
                kv, qg[a, 0, head], qg[a, 1, head], head, a, range(1, a - 1, -1), reach, factor,
                masks, biases, tuple(early_ref[kind, at : at + 1, :] for kind in range(3)),
            )
            stats_ref[0, at : at + 1, :] = top + jnp.log2(total)
            stats_ref[1, at : at + 1, :] = delta / total


def key_grads(key_block, value_block, q, g, lse, delta, masks, factor, scale):
    s = dressed(dot(key_block, q, NT), factor, 1, masks, [None] * len(masks))
    p = jnp.exp2(s - lse)
    dp = dot(value_block, g, NT)
    ds = (p * (dp - delta) * scale).astype(BF16)
    return dot(ds, q, NN), dot(p.astype(BF16), g, NN)


def stat_row(sources, kind, head, first, count):
    rows = [
        sources[a // 2][kind, 2 * head + a % 2 : 2 * head + a % 2 + 1, :]
        for a in range(first, first + count)
    ]
    return jnp.concatenate(rows, axis=1) if count > 1 else rows[0]


def query_body(reach, *refs):
    where_ref = refs[0]
    hops = reach // 2
    keys = refs[1 : 1 + 2 * (hops + 1)]
    qg_mine, qg_theirs, stats_ref, dq_mine, dq_theirs, part, kv, qg, dq, tall = refs[
        1 + 2 * (hops + 1) :
    ]
    place, pair = where_ref[0], where_ref[1]
    place_pairs(place, keys[0::2], keys[1::2], kv, 0)
    place_pairs(place, [qg_mine], [qg_theirs], qg, 0)
    heads, tokens, width = kv.shape[2:]
    scale = width ** (-0.5)
    factor = scale * LOG2E
    count = 2 * heads
    tall[...] = jnp.zeros_like(tall)
    tall[0:count] = stats_ref[0]
    tall[8 : 8 + count] = stats_ref[1]
    columns = tall[...].T
    rows = lax.broadcasted_iota(jnp.int32, (tokens, tokens), 0)
    cols = lax.broadcasted_iota(jnp.int32, (tokens, tokens), 1)
    flat = [cols > rows] + [None] * (reach - 1) + [cols <= rows]
    biases = [jnp.where(pair >= hops - hop, 0.0, NEVER) for hop in range(hops)] + [None]
    for head in range(heads):
        for a in range(2):
            at = 2 * head + a
            q, g = qg[a, 0, head], qg[a, 1, head]
            key_band = band(kv, a, reach + 1, 0, head)
            s = dressed(
                dot(q, key_band, NT), factor, 1, flat,
                [biases[j // 2] for j in range(a, a + reach + 1)],
            )
            p = jnp.exp2(s - columns[:, at : at + 1])
            dp = dot(g, band(kv, a, reach + 1, 1, head), NT)
            ds = (p * (dp - columns[:, 8 + at : 9 + at]) * scale).astype(BF16)
            dq[a, head] = dot(ds, key_band, NN).astype(BF16)
        for b in range(2):
            part[b, 0, head], part[b, 1, head] = key_grads(
                kv[b + reach, 0, head], kv[b + reach, 1, head],
                band(qg, b, 2 - b, 0, head), band(qg, b, 2 - b, 1, head),
                stat_row([stats_ref], 0, head, b, 2 - b), stat_row([stats_ref], 1, head, b, 2 - b),
                [block_mask(a - b, reach, tokens) for a in range(b, 2)], factor, scale,
            )
    dq_mine[...] = dq[place]
    dq_theirs[...] = dq[1 - place]


def later_body(reach, *refs):
    where_ref = refs[0]
    hops = reach // 2
    own_mine, own_theirs = refs[1:3]
    rows = refs[3 : 3 + 2 * hops]
    stats = refs[3 + 2 * hops : 3 + 3 * hops]
    part, mine, theirs, kv, qg, out = refs[3 + 3 * hops :]
    place = where_ref[0]
    place_pairs(place, [own_mine], [own_theirs], kv, 0)
    place_pairs(place, rows[0::2], rows[1::2], qg, 0)
    heads, tokens, width = kv.shape[2:]
    scale = width ** (-0.5)
    factor = scale * LOG2E
    for head in range(heads):
        for b in range(2):
            count = b + reach - 1
            dk, dv = key_grads(
                kv[b, 0, head], kv[b, 1, head],
                band(qg, 0, count, 0, head), band(qg, 0, count, 1, head),
                stat_row(stats, 0, head, 0, count), stat_row(stats, 1, head, 0, count),
                [block_mask(2 + at - b, reach, tokens) for at in range(count)], factor, scale,
            )
            out[b, 0, head] = (part[b, 0, head] + dk).astype(BF16)
            out[b, 1, head] = (part[b, 1, head] + dv).astype(BF16)
    mine[...] = out[place]
    theirs[...] = out[1 - place]


def lane_scalars(values, count):
    lanes = lax.broadcasted_iota(jnp.int32, (1, 128), 1)
    row = jnp.zeros((1, 128), F32)
    for at in range(count):
        row = jnp.where(lanes == at, values[at], row)
    return row


def triangle(length):
    rows = lax.broadcasted_iota(jnp.int32, (length, length), 0)
    cols = lax.broadcasted_iota(jnp.int32, (length, length), 1)
    return rows, cols


def split_decay(rows):
    high = rows.astype(BF16).astype(F32)
    lanes = lax.broadcasted_iota(jnp.int32, rows.shape, 1)
    return jnp.where(lanes < 64, high, rows - high).astype(BF16)


def joined_decay(rows):
    rows = rows.astype(F32)
    return rows + pltpu.roll(rows, 64, 1)


def summary_body(rates_ref, dy_ref, dt_ref, bc_ref, base_ref, sent_ref, cum_ref, cumt_ref, wide):
    heads, tokens, width = dy_ref.shape
    wide[...] = jnp.zeros_like(wide)
    wide[:, :heads] = dt_ref[...]
    log_decay = wide[...] * lane_scalars(rates_ref, heads)
    rows, cols = triangle(tokens)
    cum = dot((cols <= rows).astype(F32), log_decay, NN, EXACT)
    cum_ref[...] = cum
    cumt = cum.T
    cumt_ref[...] = cumt[: cumt_ref.shape[0]]
    weights = jnp.exp(cum)
    last = jnp.exp(cumt[: cumt_ref.shape[0], tokens - 1 : tokens])
    bc = bc_ref[...].astype(F32)
    for head in range(heads):
        weighted = (bc * weights[:, head : head + 1]).astype(BF16)
        state = dot(weighted, dy_ref[head], TN)[NSTATE:]
        base_ref[head * NSTATE : (head + 1) * NSTATE] = state
        sent_ref[head * NSTATE : (head + 1) * NSTATE] = state.astype(BF16)
    decay = jnp.broadcast_to(last, (last.shape[0], width))
    base_ref[heads * NSTATE :] = decay
    sent_ref[heads * NSTATE :] = split_decay(decay)


def join_body(heads, first, base_ref, *refs):
    if first:
        got_ref, far_ref, sent_ref = refs
    else:
        far_old, got_ref, far_ref, sent_ref = refs
    tail = heads * NSTATE
    got_decay = joined_decay(got_ref[tail:])
    own = base_ref[tail:]
    if first:
        far_decay = got_decay
    else:
        old_decay = far_old[tail:]
        far_decay = old_decay * got_decay
    far_ref[tail:] = far_decay
    sent_ref[tail:] = split_decay(own * far_decay)
    for head in range(heads):
        rows = slice(head * NSTATE, (head + 1) * NSTATE)
        value = got_ref[rows].astype(F32)
        if not first:
            value = far_old[rows] + old_decay[head : head + 1] * value
        far_ref[rows] = value
        sent_ref[rows] = (base_ref[rows] + own[head : head + 1] * value).astype(BF16)


def scan_body(
    rates_ref, skips_ref, u_ref, dy_ref, dt_ref, bc_ref, start_ref, far_ref, cum_ref, cumt_ref,
    du_ref, steps_ref, gbc_ref, sums_ref, wide, columns, rows_one, rows_two,
):
    heads, tokens, width = u_ref.shape
    rates = lane_scalars(rates_ref, heads)
    wide[...] = jnp.zeros_like(wide)
    wide[:, :heads] = dt_ref[...]
    dt = wide[...]
    dtt = dt.T
    columns[...] = jnp.zeros_like(columns)
    rows_one[...] = jnp.zeros_like(rows_one)
    rows_two[...] = jnp.zeros_like(rows_two)
    cum, cumt = cum_ref[...], cumt_ref[...]
    bc = bc_ref[...]
    bct = bc.astype(F32).T
    bt, ct = bct[:NSTATE], bct[NSTATE:]
    c_only = bc[:, NSTATE:]
    b_only = bc[:, :NSTATE]
    inner = dot(b_only, c_only, NT)
    s_at, t_at = triangle(tokens)
    seen = s_at <= t_at
    inner = jnp.where(seen, inner, 0.0)
    last = cum[tokens - 1 : tokens]
    tail_all = jnp.exp(last - cum)
    weights_t = jnp.exp(cumt)
    tail_t = jnp.exp(cumt[:, tokens - 1 : tokens] - cumt)
    lanes = lax.broadcasted_iota(jnp.int32, (1, 128), 1)
    whole = jnp.zeros((1, 128), F32)
    skip_sum = jnp.zeros((1, 128), F32)
    pair_sum = None
    gb_t = jnp.zeros((NSTATE, tokens), F32)
    gc_t = jnp.zeros((NSTATE, tokens), F32)
    for head in range(heads):
        u, dy = u_ref[head], dy_ref[head]
        start = start_ref[head]
        far = far_ref[head * NSTATE : (head + 1) * NSTATE]
        far_low = far.astype(BF16)
        dt_col, dt_row = dt[:, head : head + 1], dtt[head : head + 1]
        spread = cumt[head : head + 1] - cum[:, head : head + 1]
        decay = jnp.where(seen, jnp.exp(jnp.where(seen, spread, 0.0)), 0.0)
        cross = dot(u, dy, NT)
        mixing = decay * inner
        product = mixing * cross
        weighted = decay * cross * dt_col
        pair_sum = weighted if pair_sum is None else pair_sum + weighted
        columns[:, head : head + 1] = jnp.sum(product, axis=1, keepdims=True)
        from_pairs = jnp.sum(product * dt_col, axis=0, keepdims=True)
        from_start = dot(start.astype(BF16), dy, NT) * weights_t[head : head + 1]
        gc_t = gc_t + from_start
        to_far = dot(far_low, u, NT) * tail_t[head : head + 1]
        gb_t = gb_t + to_far * dt_row
        rows_one[head : head + 1] = from_pairs + jnp.sum(from_start * ct, axis=0, keepdims=True)
        rows_two[head : head + 1] = jnp.sum(to_far * bt, axis=0, keepdims=True)
        driven = dot(mixing.astype(BF16), dy, NN)
        driven = driven + tail_all[:, head : head + 1] * dot(b_only, far_low, NN)
        dy_float = dy.astype(F32)
        du_ref[head] = (dt_col * driven + skips_ref[head] * dy_float).astype(BF16)
        own_whole = jnp.sum(jnp.sum(far * start, axis=0, keepdims=True), axis=1, keepdims=True)
        whole = jnp.where(lanes == head, own_whole, whole)
        own_skip = jnp.sum(
            jnp.sum(dy_float * u.astype(F32), axis=0, keepdims=True), axis=1, keepdims=True
        )
        skip_sum = jnp.where(lanes == head, own_skip, skip_sum)
    pair_low = pair_sum.astype(BF16)
    grad_b = dot(pair_low, c_only, NN) + gb_t.T
    grad_c = dot(pair_low, b_only, TN) + gc_t.T
    gbc_ref[:, :NSTATE] = grad_b.astype(BF16)
    gbc_ref[:, NSTATE:] = grad_c.astype(BF16)
    late = rows_two[...].T
    direct = columns[...] + late
    gathered = rows_one[...].T - dt * direct
    beyond = jnp.sum(dt * late, axis=0, keepdims=True) + jnp.exp(last) * whole
    grad_log = dot(seen.astype(F32), gathered, NN, EXACT) + beyond
    steps_ref[...] = (direct + rates * grad_log).T[:heads]
    sums_ref[...] = jnp.zeros_like(sums_ref)
    sums_ref[0:1] = jnp.sum(dt * grad_log, axis=0, keepdims=True)
    sums_ref[1:2] = skip_sum


def shards(
    queries, key_vectors, values, out_grad, ssm_input, ssm_out_grad,
    step_sizes, decay_rates, skip_gains, bc_rows, saved_states,
):
    tokens, heads, width = queries.shape
    half = heads // 2
    reach = WINDOW // tokens
    hops = reach // 2
    at = lax.axis_index("seq")
    members = lax.axis_size("seq")
    place, pair = at % 2, at // 2
    where = jnp.stack([place, pair]).astype(jnp.int32)
    block = 2 * tokens * tokens * width

    sets = ssm_input.shape[1]
    held = -(-sets // 16) * 16
    u = jnp.transpose(ssm_input, (1, 0, 2))
    dy = jnp.transpose(ssm_out_grad, (1, 0, 2))
    packed = sets * NSTATE + held
    base, sent, cum, cumt = call(
        summary_body,
        [
            shape((packed, width), F32), shape((packed, width), BF16),
            shape((tokens, 128), F32), shape((held, tokens), F32),
        ],
        [decay_rates, dy, step_sizes, bc_rows],
        sets * block // 2, [pltpu.VMEM((tokens, 128), F32)], smem=1, name="summary",
    )

    def by_head(one, two):
        both = jnp.transpose(jnp.stack([one, two]), (0, 2, 1, 3))
        keep = lax.dynamic_slice_in_dim(both, place * half, half, 1)
        give = lax.dynamic_slice_in_dim(both, (1 - place) * half, half, 1)
        return keep, give

    kv_mine, kv_give = by_head(key_vectors, values)
    qg_mine, qg_give = by_head(queries, out_grad)
    kv_theirs = swapped(kv_give)
    qg_theirs = swapped(qg_give)
    keys = [(kv_mine, kv_theirs)]
    for _ in range(hops):
        keys.insert(0, tuple(moved(v, 2) for v in keys[0]))

    rows = [(qg_mine, qg_theirs), (moved(qg_mine, -2), moved(qg_theirs, -2))]
    gots = []
    far = None
    step = 1
    while step < members:
        got = moved(sent, -step)
        gots.append(got)
        if step == 2:
            base = after(base, keys[-2][1])
        if far is None:
            base = after(base, keys[-2][0], rows[1][0])
        ins = [base, got] if far is None else [base, far, got]
        far, sent = call(
            functools.partial(join_body, sets, far is None),
            [shape((packed, width), F32), shape((packed, width), BF16)],
            ins, packed * width * 4, name="join",
        )
        step *= 2
    flat = [v for both in keys for v in both]
    kv_space = pltpu.VMEM((2 * (hops + 1), 2, half, tokens, width), BF16)
    qg_space = pltpu.VMEM((2, 2, half, tokens, width), BF16)
    (early,) = call(
        functools.partial(early_body, reach),
        [shape((3, 2 * half, tokens), F32)],
        [where, *flat[2:], qg_mine, qg_theirs],
        4 * (reach - 1) * half * block, [kv_space, qg_space], smem=1, name="early",
    )
    (stats,) = call(
        functools.partial(late_body, reach),
        [shape((2, 2 * half, tokens), F32)],
        [where, *flat[:2], qg_mine, qg_theirs, early],
        6 * half * block, [qg_space, qg_space], smem=1, name="late",
    )
    later_stats = [moved(stats, -2 * (hop + 1)) for hop in range(hops)]
    far = after(far, stats)
    du, grad_steps, gbc, sums = call(
        scan_body,
        [
            shape((sets, tokens, width), BF16), shape((sets, tokens), F32),
            shape((tokens, 2 * NSTATE), BF16), shape((8, 128), F32),
        ],
        [
            decay_rates, skip_gains, u, dy, step_sizes, bc_rows,
            saved_states.reshape(saved_states.shape[1:]), far, cum, cumt,
        ],
        sets * block * 4,
        [
            pltpu.VMEM((tokens, 128), F32), pltpu.VMEM((tokens, 128), F32),
            pltpu.VMEM((128, tokens), F32), pltpu.VMEM((128, tokens), F32),
        ],
        smem=2, name="scan",
    )
    grad_inputs = jnp.transpose(du, (1, 0, 2))
    grad_steps = grad_steps.T
    gbc = lax.all_to_all(gbc, "head", 0, 0, tiled=True)
    grad_bc = jnp.sum(
        gbc.reshape(lax.axis_size("head"), -1, 2 * NSTATE).astype(F32), axis=0
    )

    dq_mine, dq_give, part = call(
        functools.partial(query_body, reach),
        [
            shape((half, tokens, width), BF16), shape((half, tokens, width), BF16),
            shape((2, 2, half, tokens, width), F32),
        ],
        [where, *flat, qg_mine, qg_theirs, stats],
        6 * (reach + 1) * half * block,
        [
            kv_space, qg_space, pltpu.VMEM((2, half, tokens, width), BF16),
            pltpu.VMEM((16, tokens), F32),
        ],
        smem=1, name="query",
    )
    dq_theirs = swapped(dq_give)
    for hop in range(1, hops):
        one, two = rows[-1]
        rows.append((moved(after(one, early), -2), moved(after(two, early), -2)))
    later = [v for both in rows[1:] for v in both]
    pair_sums = swapped(sums)
    dkv_mine, dkv_give = call(
        functools.partial(later_body, reach),
        [shape((2, half, tokens, width), BF16)] * 2,
        [where, kv_mine, kv_theirs, *later, *later_stats, part],
        8 * reach * half * block,
        [qg_space, pltpu.VMEM((2 * hops, 2, half, tokens, width), BF16), qg_space],
        smem=1, name="later",
    )
    dkv_theirs = swapped(dkv_give)

    sums = after(sums + pair_sums, dkv_give)
    pairs = members // 2
    spread = jnp.broadcast_to(sums[None], (pairs, *sums.shape))
    lines = [[2 * at + one for at in range(pairs)] for one in range(2)]
    summed = jnp.sum(
        lax.all_to_all(spread, "seq", 0, 0, axis_index_groups=lines, tiled=True), axis=0
    )
    grad_decay, grad_skip = summed[0, :sets], summed[1, :sets]

    def by_token(mine, theirs):
        first = jnp.where(place == 0, mine, theirs)
        second = jnp.where(place == 0, theirs, mine)
        return jnp.transpose(jnp.concatenate([first, second], axis=0), (1, 0, 2))

    query_grad = by_token(dq_mine, dq_theirs)
    key_grad = by_token(dkv_mine[0], dkv_theirs[0])
    value_grad = by_token(dkv_mine[1], dkv_theirs[1])
    return (
        query_grad, key_grad, value_grad, grad_inputs, grad_steps, grad_bc, grad_decay, grad_skip,
    )


def solution(mesh):
    wide = P("seq", "head", None)
    return jax.shard_map(
        shards,
        mesh=mesh,
        in_specs=(
            wide, wide, wide, wide, wide, wide, P("seq", "head"), P("head"), P("head"),
            P("seq", None), P("seq", "head", None, None),
        ),
        out_specs=(
            wide, wide, wide, wide, P("seq", "head"), P(("seq", "head"), None), P("head"), P("head"),
        ),
        check_vma=False,
    )
```
